32 devices in a mesh: dp: 16 (over z, y, x), tensor: 2 (over core).
Axes of the slice: x: 2, y: 2, z: 4, core: 2. Of those that a mesh axis runs over, the one named last changes fastest.
Arguments:
- features: bfloat16 [2048, 4096], P('dp', 'tensor'), may hold values from -6 to 6
- out_grad: bfloat16 [2048, 14336], P('dp', 'tensor'), may hold values from -0.125 to 0.125
- weight: bfloat16 [4096, 14336], P('dp', 'tensor'), may hold values from -2 to 2
- basis: bfloat16 [4096, 128], replicated, may hold values from -0.09375 to 0.09375
- moment_one: float32 [2, 7168, 128], P('tensor', 'dp'), may hold values from -3 to 3
- moment_two: float32 [2, 7168, 128], P('tensor', 'dp'), may hold values from 0.05 to 1
Outputs:
- feature_grad: bfloat16 [2048, 4096], P('dp', 'tensor')
- new_moment_one: float32 [2, 7168, 128], P('tensor', 'dp')
- new_moment_two: float32 [2, 7168, 128], P('tensor', 'dp')
- direction: float32 [2, 7168, 4096], P('tensor', 'dp')
The draws below stay inside these ranges and needn't reach their ends.
All inputs are finite; a program needn't handle non-finite values.
Results may differ from the reference program's by a relative error of at most 0.017.
Values may be sent and summed in bfloat16 or wider, within the bound.
A program may use at most 128 MiB of HBM per device.

```python
import math
import jax
import jax.numpy as jnp
from jax import lax

D = 4096
FF = 14336
R = 128
TOKENS = 2048
FF_T = 7168
N_TENSOR = 2


def steps_of(key, extent, shards, smallest, largest):
    factor_of = 1.0
    for axis_at, blocks in shards:
        heights = jax.random.uniform(jax.random.fold_in(jax.random.fold_in(key, 6), axis_at), (blocks,), jnp.float32, smallest / len(shards), largest / len(shards))
        factor_of = factor_of * jnp.repeat(jnp.exp(heights), extent[axis_at] // blocks).reshape((-1,) + (1,) * (len(extent) - 1 - axis_at))
    return factor_of


def gaussian(key, dims, deviation, limit, shards=(), dtype=jnp.bfloat16):
    entries = jax.random.normal(key, dims, jnp.float32) * deviation
    if len(shards) > 0:
        entries = steps_of(key, dims, shards, -0.22, 0.18) * entries
    return jnp.clip(entries, min=-limit, max=limit).astype(dtype)


def setup_inputs(seed: int = 0) -> dict:
    key_of = jax.random.split(jax.random.key(seed), 7)
    return {
        "features": gaussian(key_of[0], (TOKENS, D), 1.0, 6.0, ((0, 16), (1, 2))),
        "out_grad": gaussian(key_of[1], (TOKENS, FF), (TOKENS ** -0.5), 0.125, ((0, 16), (1, 2))),
        "weight": gaussian(key_of[2], (D, FF), (FF / TOKENS) ** -0.5, 2.0, ((0, 16), (1, 2))),
        "basis": gaussian(key_of[3], (D, R), D ** -0.5, 0.09375),
        "moment_one": gaussian(key_of[4], (N_TENSOR, FF_T, R), 0.5, 3.0, ((0, 2), (1, 16)), jnp.float32),
        "moment_two": jnp.clip(jnp.exp(math.log(1.0) - 2.9957323 * jax.random.uniform(key_of[5], (N_TENSOR, FF_T, R), jnp.float32) ** steps_of(key_of[5], (N_TENSOR, FF_T, R), ((0, 2), (1, 16)), -0.2, 0.2)), 0.05, 1.0),
    }


beta_one = 0.9
beta_two = 0.95
bias_one = 1.0 - 0.9 ** 20
bias_two = 1.0 - 0.95 ** 20
adam_epsilon = 1e-08

def reference(features, out_grad, weight, basis, moment_one, moment_two):
    block_width = FF // N_TENSOR
    total = jnp.zeros((features.shape[0], D), jnp.float32)
    for block in range(N_TENSOR):
        grad_block = out_grad[:, block * block_width:(block + 1) * block_width]
        weight_block = weight[:, block * block_width:(block + 1) * block_width]
        part = jnp.dot(grad_block, weight_block.T, preferred_element_type=jnp.float32)
        total = total + lax.optimization_barrier(part.astype(jnp.bfloat16)).astype(jnp.float32)
    feature_grad = total.astype(jnp.bfloat16)
    coords = jnp.dot(features, basis, preferred_element_type=jnp.float32).astype(jnp.bfloat16)
    projected = jnp.dot(out_grad.T, coords, preferred_element_type=jnp.float32)
    projected = projected.reshape(N_TENSOR, block_width, R)
    new_one = beta_one * moment_one + (1.0 - beta_one) * projected
    new_two = beta_two * moment_two + (1.0 - beta_two) * projected * projected
    step_dir = (new_one / bias_one / (jnp.sqrt(new_two / bias_two) + adam_epsilon)).astype(jnp.bfloat16)
    direction = jnp.dot(step_dir.reshape(FF, R), basis.T, preferred_element_type=jnp.float32)
    return (feature_grad, new_one, new_two, direction.reshape(N_TENSOR, block_width, D))
```

```python
import functools

import jax
import jax.numpy as jnp
from jax import lax
from jax.experimental import pallas as pl
from jax.experimental.pallas import tpu as pltpu
from jax.sharding import PartitionSpec as P

beta_one = 0.9
beta_two = 0.95
bias_one = 1.0 - 0.9**20
bias_two = 1.0 - 0.95**20
adam_epsilon = 1e-08

MESH = pl.DeviceIdType.MESH
SQUARE = 4
PARTS = 2
LANES = 1024
NT = (((1,), (1,)), ((), ()))
TN = (((0,), (0,)), ((), ()))


def exchange_kernel(
    line, n_tensor,
    features, out_grad, weight, basis,
    grad_out, projected_out,
    tokens, rows, coords, coords_part, tiles, pair_tiles, final_tiles, proj, proj_send, proj_recv,
    local_sem, line_send, line_recv, row_send, row_recv, far_send, far_recv,
    part_send, part_recv, coords_send, coords_recv,
    proj_send_sem, proj_recv_sem, pair_send, pair_recv, final_send, final_recv,
):
    me = lax.axis_index("dp")
    core = lax.axis_index("tensor")
    place = me // SQUARE
    corner = me % SQUARE
    side_x = place * SQUARE + corner + 1 - 2 * (corner % 2)
    side_y = place * SQUARE + corner + 2 - 4 * (corner // 2)
    far = place * SQUARE + (SQUARE - 1 - corner)
    other = 1 - core
    n_tok = out_grad.shape[0]
    width = out_grad.shape[1]
    n_row = weight.shape[0]
    half = n_row // 2
    piece = n_tok // PARTS
    own = line // n_tensor

    def on_line(z):
        return z * SQUARE + corner

    def remote(src, dst, send, recv, dp, tensor):
        return pltpu.make_async_remote_copy(
            src_ref=src, dst_ref=dst, send_sem=send, recv_sem=recv,
            device_id=(dp, tensor), device_id_type=MESH,
        )

    def arrived(dst, sem):
        remote(dst, dst, sem, sem, me, other).wait_recv()

    def token_piece(z, p):
        return tokens.at[pl.ds(pl.multiple_of(z * n_tok + p * piece, piece), piece), :]

    keep_tokens = pltpu.make_async_copy(
        out_grad, tokens.at[pl.ds(pl.multiple_of(place * n_tok, n_tok), n_tok), :], local_sem.at[0]
    )
    keep_rows = pltpu.make_async_copy(weight, rows.at[0], local_sem.at[1])
    keep_tokens.start()
    keep_rows.start()

    barrier = pltpu.get_barrier_semaphore()
    greeted = [(me, other), (side_x, core), (side_y, core), (far, core)]
    for s in range(1, line):
        for t in range(n_tensor):
            greeted.append((on_line((place + s) % line), t))
    for dp, t in greeted:
        pl.semaphore_signal(barrier, inc=1, device_id=(dp, t), device_id_type=MESH)
    pl.semaphore_wait(barrier, len(greeted))

    def line_copy(src, z, p, way):
        target = on_line(place + 1 if way == 0 else place - 1)
        return remote(
            src, token_piece(z, p), line_send.at[way, z, p], line_recv.at[z, p], target, core
        )

    for p in range(PARTS):
        for way, there in ((0, place + 1 < line), (1, place > 0)):
            @pl.when(there)
            def _():
                line_copy(out_grad.at[pl.ds(p * piece, piece), :], place, p, way).start()

    def row_copy(slot, h):
        return remote(
            weight.at[pl.ds(h * half, half), :],
            rows.at[slot, pl.ds(h * half, half), :],
            row_send.at[slot - 1, h], row_recv.at[slot - 1, h],
            side_x if slot == 1 else side_y, core,
        )

    def far_copy(h):
        src = rows.at[1 + h, pl.ds(h * half, half), :]
        return remote(
            src, rows.at[3, pl.ds(h * half, half), :], far_send.at[h], far_recv.at[h],
            side_y if h == 0 else side_x, core,
        )

    for slot, h in ((1, 0), (2, 1), (1, 1), (2, 0)):
        row_copy(slot, h).start()

    depth = features.shape[1]
    coords_part[0] = jnp.dot(
        features[...],
        basis[pl.ds(pl.multiple_of(core * depth, depth), depth), :],
        preferred_element_type=jnp.float32,
    )
    part_copy = remote(
        coords_part.at[0], coords_part.at[1], part_send.at[0], part_recv.at[0], me, other
    )
    part_copy.start()
    part_copy.wait()
    coords[place] = (coords_part[0] + coords_part[1]).astype(coords.dtype)

    def coords_copy(s):
        z = (place + s) % line
        return remote(
            coords.at[place], coords.at[place], coords_send.at[s], coords_recv.at[place],
            on_line(z), core,
        )

    for s in range(1, line):
        coords_copy(s).start()
    keep_tokens.wait()
    keep_rows.wait()

    strip = SQUARE * projected_out.shape[0]

    def add_projected(z, first=False):
        block = tokens[
            pl.ds(pl.multiple_of(z * n_tok, n_tok), n_tok),
            pl.ds(pl.multiple_of(place * strip, strip), strip),
        ]
        term = lax.dot_general(block, coords[z], TN, preferred_element_type=jnp.float32)
        proj[...] = term if first else proj[...] + term

    def product(first_token, count, slot):
        def step(k, total):
            at = pl.ds(pl.multiple_of(k * LANES, LANES), LANES)
            return total + lax.dot_general(
                tokens[pl.ds(first_token, count), at], rows[slot, :, at], NT,
                preferred_element_type=jnp.float32,
            )

        start = jnp.zeros((count, n_row), jnp.float32)
        return lax.fori_loop(0, width // LANES, step, start)

    def column(slot):
        flip_x = slot % 2
        flip_y = slot // 2
        x, y = corner % 2, corner // 2
        return (x + flip_x) % 2 + 2 * ((y + flip_y) % 2)

    def tile(z, slot):
        got = product(pl.multiple_of(z * n_tok, n_tok), n_tok, slot)
        tiles[z, column(slot)] = got.astype(tiles.dtype)

    def tiles_of(z, slots):
        def one(slot, carry):
            tile(z, slot)
            return carry

        lax.fori_loop(slots[0], slots[1], one, 0)

    add_projected(place, first=True)
    tile(place, 0)

    late = max(line - 2, 1)
    for s in range(1, line):
        from_left = place - s >= 0
        from_right = place + s < line
        for p in range(PARTS):
            for way, here, z, on in (
                (0, from_left, place - s, place + 1 < line),
                (1, from_right, place + s, place > 0),
            ):
                @pl.when(here)
                def _():
                    arrived(token_piece(z, p), line_recv.at[z, p])

                    @pl.when(on)
                    def _():
                        line_copy(token_piece(z, p), z, p, way).start()

        if s == 1:
            for h in range(2):
                arrived(rows.at[1 + h, pl.ds(h * half, half), :], row_recv.at[h, h])
                far_copy(h).start()

        for here, z in ((from_left, place - s), (from_right, place + s)):
            @pl.when(here)
            def _():
                arrived(coords.at[z], coords_recv.at[z])
                add_projected(z)

        if s == line - 1:
            for r in range(SQUARE):
                proj_send[r] = proj[
                    pl.ds(r * projected_out.shape[0], projected_out.shape[0]), :
                ].astype(proj_send.dtype)
            for r, dp in ((1, side_x), (2, side_y), (3, far)):
                remote(
                    proj_send.at[dp - place * SQUARE], proj_recv.at[r - 1],
                    proj_send_sem.at[r - 1], proj_recv_sem.at[r - 1], dp, core,
                ).start()

        for here, z in ((from_left, place - s), (from_right, place + s)):
            @pl.when(here)
            def _():
                tiles_of(z, (0, 3 if s > late else 1))

        if s == late:
            for h in range(2):
                arrived(
                    rows.at[1 + h, pl.ds((1 - h) * half, half), :], row_recv.at[h, 1 - h]
                )

            def early(z, carry):
                @pl.when((z - place <= late) & (place - z <= late))
                def _():
                    tiles_of(z, (1, 3))

                return carry

            lax.fori_loop(0, line, early, 0)

    for h in range(2):
        arrived(rows.at[3, pl.ds(h * half, half), :], far_recv.at[h])

    def last(z, carry):
        tile(z, 3)
        return carry

    def last_other(i, carry):
        return last(other * own + i, carry)

    def last_own(i, carry):
        return last(core * own + i, carry)

    pair_copies = [
        remote(
            tiles.at[other * own + i], pair_tiles.at[i], pair_send.at[i], pair_recv.at[i], me, other
        )
        for i in range(own)
    ]
    lax.fori_loop(0, own, last_other, 0)
    for copy in pair_copies:
        copy.start()
    lax.fori_loop(0, own, last_own, 0)

    mine = place // own
    for i in range(own):
        pair_copies[i].wait_recv()
        z = core * own + i
        pair_tiles[i] = (
            tiles[z].astype(jnp.float32) + pair_tiles[i].astype(jnp.float32)
        ).astype(pair_tiles.dtype)

        @pl.when(z == place)
        def _():
            final_tiles[place % own] = pair_tiles[i]

        @pl.when(z != place)
        def _():
            remote(
                pair_tiles.at[i], final_tiles.at[place % own],
                final_send.at[i], final_recv.at[place % own], on_line(z), mine,
            ).start()

    count = projected_out.shape[0]
    total = proj[pl.ds(pl.multiple_of(corner * count, count), count), :]
    for r in range(3):
        arrived(proj_recv.at[r], proj_recv_sem.at[r])
        total = total + proj_recv[r].astype(jnp.float32)
    projected_out[...] = total

    for i in range(own):
        @pl.when(core * own + i != place)
        def _():
            arrived(final_tiles.at[i], final_recv.at[i])

        for c in range(SQUARE):
            at = (i * SQUARE + c) * n_row
            grad_out[:, pl.ds(at, n_row)] = final_tiles[i, c]

    for s in range(1, line):
        coords_copy(s).wait_send()
    for slot in (1, 2):
        for h in range(2):
            row_copy(slot, h).wait_send()
    for h in range(2):
        far_copy(h).wait_send()
    for s in range(line):
        for p in range(PARTS):
            for way, here, z, on in (
                (0, place - s >= 0, place - s, place + 1 < line),
                (1, place + s < line, place + s, place > 0),
            ):
                @pl.when(here & on)
                def _():
                    line_copy(token_piece(z, p), z, p, way).wait_send()
    for r, dp in ((1, side_x), (2, side_y), (3, far)):
        remote(
            proj_send.at[dp - place * SQUARE], proj_recv.at[r - 1],
            proj_send_sem.at[r - 1], proj_recv_sem.at[r - 1], dp, core,
        ).wait_send()
    for i in range(own):
        pair_copies[i].wait_send()

        @pl.when(core * own + i != place)
        def _():
            remote(
                pair_tiles.at[i], final_tiles.at[place % own],
                final_send.at[i], final_recv.at[place % own], on_line(core * own + i), mine,
            ).wait_send()


def adam_kernel(projected, moment_one, moment_two, basis, new_one, new_two, direction, step_dir):
    @pl.when(pl.program_id(0) == 0)
    def _():
        value = projected[...]
        one = beta_one * moment_one[...] + (1.0 - beta_one) * value
        two = beta_two * moment_two[...] + (1.0 - beta_two) * value * value
        new_one[...] = one
        new_two[...] = two
        step_dir[...] = (
            one / bias_one / (jnp.sqrt(two / bias_two) + adam_epsilon)
        ).astype(step_dir.dtype)

    direction[...] = lax.dot_general(
        step_dir[...], basis[...], NT, preferred_element_type=jnp.float32
    )


def fused_body(n_dp, n_tensor, features, out_grad, weight, basis, moment_one, moment_two):
    line = n_dp // SQUARE
    own = line // n_tensor
    n_tok, width = out_grad.shape
    n_row = weight.shape[0]
    units, rank = moment_one.shape[1:]
    dma = pltpu.SemaphoreType.DMA
    bf16, f32 = jnp.bfloat16, jnp.float32
    feature_grad, projected = pl.pallas_call(
        functools.partial(exchange_kernel, line, n_tensor),
        out_shape=(
            jax.ShapeDtypeStruct(features.shape, bf16),
            jax.ShapeDtypeStruct((units, rank), f32),
        ),
        in_specs=[
            pl.BlockSpec(memory_space=pltpu.VMEM),
            pl.BlockSpec(memory_space=pl.ANY),
            pl.BlockSpec(memory_space=pl.ANY),
            pl.BlockSpec(memory_space=pltpu.VMEM),
        ],
        out_specs=[pl.BlockSpec(memory_space=pltpu.VMEM)] * 2,
        scratch_shapes=[
            pltpu.VMEM((line * n_tok, width), bf16),
            pltpu.VMEM((SQUARE, n_row, width), bf16),
            pltpu.VMEM((line, n_tok, rank), bf16),
            pltpu.VMEM((2, n_tok, rank), f32),
            pltpu.VMEM((line, SQUARE, n_tok, n_row), bf16),
            pltpu.VMEM((own, SQUARE, n_tok, n_row), bf16),
            pltpu.VMEM((own, SQUARE, n_tok, n_row), bf16),
            pltpu.VMEM((SQUARE * units, rank), f32),
            pltpu.VMEM((SQUARE, units, rank), bf16),
            pltpu.VMEM((SQUARE - 1, units, rank), bf16),
            dma((2,)),
            dma((2, line, PARTS)),
            dma((line, PARTS)),
            dma((2, 2)),
            dma((2, 2)),
            dma((2,)),
            dma((2,)),
            dma((1,)),
            dma((1,)),
            dma((line,)),
            dma((line,)),
            dma((SQUARE - 1,)),
            dma((SQUARE - 1,)),
            dma((own,)),
            dma((own,)),
            dma((own,)),
            dma((own,)),
        ],
        compiler_params=pltpu.CompilerParams(
            collective_id=0, has_side_effects=True, vmem_limit_bytes=48 << 20
        ),
        name="exchange",
    )(features, out_grad, weight, basis)

    n_feature = basis.shape[0]
    block = min(512, n_feature)
    whole = pl.BlockSpec((units, rank), lambda i: (0, 0))
    new_one, new_two, direction = pl.pallas_call(
        adam_kernel,
        grid=(n_feature // block,),
        out_shape=(
            jax.ShapeDtypeStruct((units, rank), f32),
            jax.ShapeDtypeStruct((units, rank), f32),
            jax.ShapeDtypeStruct((units, n_feature), f32),
        ),
        in_specs=[whole, whole, whole, pl.BlockSpec((block, rank), lambda i: (i, 0))],
        out_specs=[whole, whole, pl.BlockSpec((units, block), lambda i: (0, i))],
        scratch_shapes=[pltpu.VMEM((units, rank), bf16)],
        name="adam",
    )(projected, moment_one[0], moment_two[0], basis)
    return (feature_grad, new_one[None], new_two[None], direction[None])


def gathered_body(features, out_grad, weight, basis, moment_one, moment_two):
    partial_value = jnp.einsum(
        "tf,df->td",
        out_grad,
        lax.all_gather(weight, "dp", axis=0, tiled=True),
        preferred_element_type=jnp.float32,
    )
    feature_grad = lax.psum_scatter(
        partial_value.astype(jnp.bfloat16), "tensor", scatter_dimension=1, tiled=True
    )
    part_width = features.shape[1]
    basis_part = lax.dynamic_slice_in_dim(
        basis, lax.axis_index("tensor") * part_width, part_width, 0
    )
    local_coords = jnp.dot(features, basis_part, preferred_element_type=jnp.float32)
    coords = lax.psum(local_coords, "tensor")
    coords = coords.astype(jnp.bfloat16)
    projected = lax.psum_scatter(
        jnp.einsum("tf,tr->fr", out_grad, coords, preferred_element_type=jnp.float32),
        "dp",
        scatter_dimension=0,
        tiled=True,
    )
    first = moment_one[0]
    second = moment_two[0]
    new_one = beta_one * first + (1.0 - beta_one) * projected
    new_two = beta_two * second + (1.0 - beta_two) * projected * projected
    step_dir = (new_one / bias_one / (jnp.sqrt(new_two / bias_two) + adam_epsilon)).astype(
        jnp.bfloat16
    )
    direction = jnp.einsum("cr,dr->cd", step_dir, basis, preferred_element_type=jnp.float32)
    return (feature_grad, new_one[None], new_two[None], direction[None])


def body(n_dp, n_tensor, *arrays):
    features, out_grad, weight, _, moment_one, _ = arrays
    line = n_dp // SQUARE
    units = moment_one.shape[1]
    fits = (
        n_tensor == 2
        and n_dp % SQUARE == 0
        and line % n_tensor == 0
        and out_grad.shape[1] % LANES == 0
        and out_grad.shape[0] % (16 * PARTS) == 0
        and weight.shape[0] % 128 == 0
        and units % 16 == 0
        and (units * SQUARE) % 128 == 0
    )
    if fits:
        return fused_body(n_dp, n_tensor, *arrays)
    return gathered_body(*arrays)


def solution(mesh):
    in_specs = (
        P("dp", "tensor"),
        P("dp", "tensor"),
        P("dp", "tensor"),
        P(),
        P("tensor", "dp", None),
        P("tensor", "dp", None),
    )
    out_specs = (
        P("dp", "tensor"),
        P("tensor", "dp", None),
        P("tensor", "dp", None),
        P("tensor", "dp", None),
    )
    run = functools.partial(body, mesh.shape["dp"], mesh.shape["tensor"])
    return jax.shard_map(run, mesh=mesh, in_specs=in_specs, out_specs=out_specs, check_vma=False)
```

```python
import functools

import jax
import jax.numpy as jnp
from jax import lax
from jax.experimental import pallas as pl
from jax.experimental.pallas import tpu as pltpu
from jax.sharding import PartitionSpec as P

beta_one = 0.9
beta_two = 0.95
bias_one = 1.0 - 0.9**20
bias_two = 1.0 - 0.95**20
adam_epsilon = 1e-08

MESH = pl.DeviceIdType.MESH
SQUARE = 4
PARTS = 2
LANES = 1024
NT = (((1,), (1,)), ((), ()))
TN = (((0,), (0,)), ((), ()))


def moments(projected, moment_one, moment_two):
    return (
        beta_one * moment_one + (1.0 - beta_one) * projected,
        beta_two * moment_two + (1.0 - beta_two) * projected * projected,
    )


def exchange_kernel(
    line, n_tensor,
    features_in, out_grad, weight, basis_in, moment_one_in, moment_two_in,
    grad_out, projected_out, step_out,
    features, basis, moment_one, moment_two, tokens, rows, coords, coords_part, tiles, pair_tiles, final_tiles, proj, proj_send, proj_recv,
    local_sem, line_send, line_recv, row_send, row_recv, far_send, far_recv,
    part_send, part_recv, coords_send, coords_recv,
    proj_send_sem, proj_recv_sem, pair_send, pair_recv, final_send, final_recv,
):
    me = lax.axis_index("dp")
    core = lax.axis_index("tensor")
    place = me // SQUARE
    corner = me % SQUARE
    side_x = place * SQUARE + corner + 1 - 2 * (corner % 2)
    side_y = place * SQUARE + corner + 2 - 4 * (corner // 2)
    far = place * SQUARE + (SQUARE - 1 - corner)
    other = 1 - core
    n_tok = out_grad.shape[0]
    width = out_grad.shape[1]
    n_row = weight.shape[0]
    quarter = n_row // 4
    piece = n_tok // PARTS
    own = line // n_tensor

    def on_line(z):
        return z * SQUARE + corner

    def remote(src, dst, send, recv, dp, tensor):
        return pltpu.make_async_remote_copy(
            src_ref=src, dst_ref=dst, send_sem=send, recv_sem=recv,
            device_id=(dp, tensor), device_id_type=MESH,
        )

    def arrived(dst, sem):
        remote(dst, dst, sem, sem, me, other).wait_recv()

    def token_piece(z, p):
        return tokens.at[pl.ds(pl.multiple_of(z * n_tok + p * piece, piece), piece), :]

    keep_tokens = pltpu.make_async_copy(
        out_grad, tokens.at[pl.ds(pl.multiple_of(place * n_tok, n_tok), n_tok), :], local_sem.at[0]
    )
    keep_rows = pltpu.make_async_copy(weight, rows.at[0], local_sem.at[1])
    loads = [
        pltpu.make_async_copy(src, dst, local_sem.at[2 + i])
        for i, (src, dst) in enumerate(
            (
                (features_in, features),
                (basis_in, basis),
                (moment_one_in, moment_one),
                (moment_two_in, moment_two),
            )
        )
    ]
    for load in loads[:2]:
        load.start()
    keep_tokens.start()
    keep_rows.start()
    for load in loads[2:]:
        load.start()

    barrier = pltpu.get_barrier_semaphore()
    greeted = [(me, other), (side_x, core), (side_y, core), (far, core)]
    for s in range(1, line):
        for t in range(n_tensor):
            greeted.append((on_line((place + s) % line), t))
    for dp, t in greeted:
        pl.semaphore_signal(barrier, inc=1, device_id=(dp, t), device_id_type=MESH)
    pl.semaphore_wait(barrier, len(greeted))

    def line_copy(src, z, p, way):
        target = on_line(place + 1 if way == 0 else place - 1)
        return remote(
            src, token_piece(z, p), line_send.at[way, z, p], line_recv.at[z, p], target, core
        )

    for p in range(PARTS):
        for way, there in ((0, place + 1 < line), (1, place > 0)):
            @pl.when(there)
            def _():
                line_copy(out_grad.at[pl.ds(p * piece, piece), :], place, p, way).start()

    def row_copy(slot, k):
        return remote(
            weight.at[pl.ds(k * quarter, quarter), :],
            rows.at[slot, pl.ds(k * quarter, quarter), :],
            row_send.at[slot - 1, k], row_recv.at[slot - 1, k],
            side_x if slot == 1 else side_y, core,
        )

    def far_copy(k):
        src = rows.at[1 + k // 2, pl.ds(k * quarter, quarter), :]
        return remote(
            src, rows.at[3, pl.ds(k * quarter, quarter), :], far_send.at[k], far_recv.at[k],
            side_y if k < 2 else side_x, core,
        )

    for slot, k in ((1, 0), (2, 2), (1, 1), (2, 3), (1, 2), (2, 0)):
        row_copy(slot, k).start()

    depth = features.shape[1]
    loads[0].wait()
    loads[1].wait()
    coords_part[0] = jnp.dot(
        features[...],
        basis[pl.ds(pl.multiple_of(core * depth, depth), depth), :],
        preferred_element_type=jnp.float32,
    )
    part_copy = remote(
        coords_part.at[0], coords_part.at[1], part_send.at[0], part_recv.at[0], me, other
    )
    part_copy.start()
    part_copy.wait()
    coords[place] = (coords_part[0] + coords_part[1]).astype(coords.dtype)

    def coords_copy(s):
        z = (place + s) % line
        return remote(
            coords.at[place], coords.at[place], coords_send.at[s], coords_recv.at[place],
            on_line(z), core,
        )

    for s in range(1, line):
        coords_copy(s).start()
    keep_tokens.wait()
    keep_rows.wait()

    strip = SQUARE * projected_out.shape[0]

    def add_projected(z, first=False):
        block = tokens[
            pl.ds(pl.multiple_of(z * n_tok, n_tok), n_tok),
            pl.ds(pl.multiple_of(place * strip, strip), strip),
        ]
        term = lax.dot_general(block, coords[z], TN, preferred_element_type=jnp.float32)
        proj[...] = term if first else proj[...] + term

    def product(first_token, count, slot):
        def step(k, total):
            at = pl.ds(pl.multiple_of(k * LANES, LANES), LANES)
            return total + lax.dot_general(
                tokens[pl.ds(first_token, count), at], rows[slot, :, at], NT,
                preferred_element_type=jnp.float32,
            )

        start = jnp.zeros((count, n_row), jnp.float32)
        return lax.fori_loop(0, width // LANES, step, start)

    def column(slot):
        flip_x = slot % 2
        flip_y = slot // 2
        x, y = corner % 2, corner // 2
        return (x + flip_x) % 2 + 2 * ((y + flip_y) % 2)

    def tile(z, slot):
        got = product(pl.multiple_of(z * n_tok, n_tok), n_tok, slot)
        tiles[z, column(slot)] = got.astype(tiles.dtype)

    def tiles_of(z, slots):
        def one(slot, carry):
            tile(z, slot)
            return carry

        lax.fori_loop(slots[0], slots[1], one, 0)

    add_projected(place, first=True)
    tile(place, 0)

    late = max(line - 2, 1)
    for s in range(1, line):
        from_left = place - s >= 0
        from_right = place + s < line
        for p in range(PARTS):
            for way, here, z, on in (
                (0, from_left, place - s, place + 1 < line),
                (1, from_right, place + s, place > 0),
            ):
                @pl.when(here)
                def _():
                    arrived(token_piece(z, p), line_recv.at[z, p])

                    @pl.when(on)
                    def _():
                        line_copy(token_piece(z, p), z, p, way).start()

        if s == 1:
            row_copy(1, 3).start()
            row_copy(2, 1).start()
        if s == late:
            for k in (0, 2, 1, 3):
                slot = 1 + k // 2
                arrived(rows.at[slot, pl.ds(k * quarter, quarter), :], row_recv.at[slot - 1, k])
                far_copy(k).start()

        for here, z in ((from_left, place - s), (from_right, place + s)):
            @pl.when(here)
            def _():
                arrived(coords.at[z], coords_recv.at[z])
                add_projected(z)

        if s == line - 1:
            for r in range(SQUARE):
                proj_send[r] = proj[
                    pl.ds(r * projected_out.shape[0], projected_out.shape[0]), :
                ].astype(proj_send.dtype)
            for r, dp in ((1, side_x), (2, side_y), (3, far)):
                remote(
                    proj_send.at[dp - place * SQUARE], proj_recv.at[r - 1],
                    proj_send_sem.at[r - 1], proj_recv_sem.at[r - 1], dp, core,
                ).start()

        for here, z in ((from_left, place - s), (from_right, place + s)):
            @pl.when(here)
            def _():
                tiles_of(z, (0, 3 if s > late else 1))

        if s == late:
            for slot, k in ((1, 2), (2, 0), (1, 3), (2, 1)):
                arrived(rows.at[slot, pl.ds(k * quarter, quarter), :], row_recv.at[slot - 1, k])

            def early(z, carry):
                @pl.when((z - place <= late) & (place - z <= late))
                def _():
                    tiles_of(z, (1, 3))

                return carry

            lax.fori_loop(0, line, early, 0)

    for k in range(4):
        arrived(rows.at[3, pl.ds(k * quarter, quarter), :], far_recv.at[k])

    def last(t):
        got = product(pl.multiple_of(t * own * n_tok, own * n_tok), own * n_tok, 3)
        for i in range(own):
            tiles[t * own + i, column(3)] = got[i * n_tok : (i + 1) * n_tok].astype(tiles.dtype)

    pair_copies = [
        remote(
            tiles.at[other * own + i], pair_tiles.at[i], pair_send.at[i], pair_recv.at[i], me, other
        )
        for i in range(own)
    ]
    last(other)
    for copy in pair_copies:
        copy.start()
    last(core)

    mine = place // own
    for i in range(own):
        pair_copies[i].wait_recv()
        z = core * own + i
        pair_tiles[i] = (
            tiles[z].astype(jnp.float32) + pair_tiles[i].astype(jnp.float32)
        ).astype(pair_tiles.dtype)

        @pl.when(z == place)
        def _():
            final_tiles[place % own] = pair_tiles[i]

        @pl.when(z != place)
        def _():
            remote(
                pair_tiles.at[i], final_tiles.at[place % own],
                final_send.at[i], final_recv.at[place % own], on_line(z), mine,
            ).start()

    count = projected_out.shape[0]
    total = proj[pl.ds(pl.multiple_of(corner * count, count), count), :]
    for r in range(3):
        arrived(proj_recv.at[r], proj_recv_sem.at[r])
        total = total + proj_recv[r].astype(jnp.float32)
    projected_out[...] = total
    loads[2].wait()
    loads[3].wait()
    one, two = moments(total, moment_one[...], moment_two[...])
    step_out[...] = (
        one / bias_one / (jnp.sqrt(two / bias_two) + adam_epsilon)
    ).astype(step_out.dtype)

    for i in range(own):
        @pl.when(core * own + i != place)
        def _():
            arrived(final_tiles.at[i], final_recv.at[i])

        for c in range(SQUARE):
            at = (i * SQUARE + c) * n_row
            grad_out[:, pl.ds(at, n_row)] = final_tiles[i, c]

    for s in range(1, line):
        coords_copy(s).wait_send()
    for slot in (1, 2):
        for k in range(4):
            row_copy(slot, k).wait_send()
    for k in range(4):
        far_copy(k).wait_send()
    for s in range(line):
        for p in range(PARTS):
            for way, here, z, on in (
                (0, place - s >= 0, place - s, place + 1 < line),
                (1, place + s < line, place + s, place > 0),
            ):
                @pl.when(here & on)
                def _():
                    line_copy(token_piece(z, p), z, p, way).wait_send()
    for r, dp in ((1, side_x), (2, side_y), (3, far)):
        remote(
            proj_send.at[dp - place * SQUARE], proj_recv.at[r - 1],
            proj_send_sem.at[r - 1], proj_recv_sem.at[r - 1], dp, core,
        ).wait_send()
    for i in range(own):
        pair_copies[i].wait_send()

        @pl.when(core * own + i != place)
        def _():
            remote(
                pair_tiles.at[i], final_tiles.at[place % own],
                final_send.at[i], final_recv.at[place % own], on_line(core * own + i), mine,
            ).wait_send()


def direction_kernel(step_dir, projected, moment_one, moment_two, basis, new_one, new_two, direction):
    direction[...] = lax.dot_general(
        step_dir[...], basis[...], NT, preferred_element_type=jnp.float32
    )

    @pl.when(pl.program_id(0) == 1)
    def _():
        new_one[...], new_two[...] = moments(projected[...], moment_one[...], moment_two[...])


def fused_body(n_dp, n_tensor, features, out_grad, weight, basis, moment_one, moment_two):
    line = n_dp // SQUARE
    own = line // n_tensor
    n_tok, width = out_grad.shape
    n_row = weight.shape[0]
    units, rank = moment_one.shape[1:]
    dma = pltpu.SemaphoreType.DMA
    bf16, f32 = jnp.bfloat16, jnp.float32
    feature_grad, projected, step_dir = pl.pallas_call(
        functools.partial(exchange_kernel, line, n_tensor),
        out_shape=(
            jax.ShapeDtypeStruct(features.shape, bf16),
            jax.ShapeDtypeStruct((units, rank), f32),
            jax.ShapeDtypeStruct((units, rank), bf16),
        ),
        in_specs=[pl.BlockSpec(memory_space=pltpu.HBM)] * 6,
        out_specs=[pl.BlockSpec(memory_space=pltpu.VMEM)] * 3,
        scratch_shapes=[
            pltpu.VMEM(features.shape, bf16),
            pltpu.VMEM(basis.shape, bf16),
            pltpu.VMEM((units, rank), f32),
            pltpu.VMEM((units, rank), f32),
            pltpu.VMEM((line * n_tok, width), bf16),
            pltpu.VMEM((SQUARE, n_row, width), bf16),
            pltpu.VMEM((line, n_tok, rank), bf16),
            pltpu.VMEM((2, n_tok, rank), f32),
            pltpu.VMEM((line, SQUARE, n_tok, n_row), bf16),
            pltpu.VMEM((own, SQUARE, n_tok, n_row), bf16),
            pltpu.VMEM((own, SQUARE, n_tok, n_row), bf16),
            pltpu.VMEM((SQUARE * units, rank), f32),
            pltpu.VMEM((SQUARE, units, rank), bf16),
            pltpu.VMEM((SQUARE - 1, units, rank), bf16),
            dma((6,)),
            dma((2, line, PARTS)),
            dma((line, PARTS)),
            dma((2, 4)),
            dma((2, 4)),
            dma((4,)),
            dma((4,)),
            dma((1,)),
            dma((1,)),
            dma((line,)),
            dma((line,)),
            dma((SQUARE - 1,)),
            dma((SQUARE - 1,)),
            dma((own,)),
            dma((own,)),
            dma((own,)),
            dma((own,)),
        ],
        compiler_params=pltpu.CompilerParams(
            collective_id=0, has_side_effects=True, vmem_limit_bytes=64 << 20
        ),
        name="exchange",
    )(features, out_grad, weight, basis, moment_one[0], moment_two[0])

    n_feature = basis.shape[0]
    block = n_feature // 4
    whole = pl.BlockSpec((units, rank), lambda i: (0, 0))
    new_one, new_two, direction = pl.pallas_call(
        direction_kernel,
        grid=(n_feature // block,),
        out_shape=(
            jax.ShapeDtypeStruct((units, rank), f32),
            jax.ShapeDtypeStruct((units, rank), f32),
            jax.ShapeDtypeStruct((units, n_feature), f32),
        ),
        in_specs=[whole, whole, whole, whole, pl.BlockSpec((block, rank), lambda i: (i, 0))],
        out_specs=[whole, whole, pl.BlockSpec((units, block), lambda i: (0, i))],
        compiler_params=pltpu.CompilerParams(vmem_limit_bytes=64 << 20),
        name="direction",
    )(step_dir, projected, moment_one[0], moment_two[0], basis)
    return (feature_grad, new_one[None], new_two[None], direction[None])


def gathered_body(features, out_grad, weight, basis, moment_one, moment_two):
    partial_value = jnp.einsum(
        "tf,df->td",
        out_grad,
        lax.all_gather(weight, "dp", axis=0, tiled=True),
        preferred_element_type=jnp.float32,
    )
    feature_grad = lax.psum_scatter(
        partial_value.astype(jnp.bfloat16), "tensor", scatter_dimension=1, tiled=True
    )
    part_width = features.shape[1]
    basis_part = lax.dynamic_slice_in_dim(
        basis, lax.axis_index("tensor") * part_width, part_width, 0
    )
    local_coords = jnp.dot(features, basis_part, preferred_element_type=jnp.float32)
    coords = lax.psum(local_coords, "tensor")
    coords = coords.astype(jnp.bfloat16)
    projected = lax.psum_scatter(
        jnp.einsum("tf,tr->fr", out_grad, coords, preferred_element_type=jnp.float32),
        "dp",
        scatter_dimension=0,
        tiled=True,
    )
    first = moment_one[0]
    second = moment_two[0]
    new_one = beta_one * first + (1.0 - beta_one) * projected
    new_two = beta_two * second + (1.0 - beta_two) * projected * projected
    step_dir = (new_one / bias_one / (jnp.sqrt(new_two / bias_two) + adam_epsilon)).astype(
        jnp.bfloat16
    )
    direction = jnp.einsum("cr,dr->cd", step_dir, basis, preferred_element_type=jnp.float32)
    return (feature_grad, new_one[None], new_two[None], direction[None])


def body(n_dp, n_tensor, *arrays):
    _, out_grad, weight, basis, moment_one, _ = arrays
    line = n_dp // SQUARE
    units = moment_one.shape[1]
    fits = (
        n_tensor == 2
        and n_dp % SQUARE == 0
        and line % n_tensor == 0
        and out_grad.shape[1] % LANES == 0
        and out_grad.shape[0] % (16 * PARTS) == 0
        and weight.shape[0] % 128 == 0
        and units % 16 == 0
        and basis.shape[0] % 512 == 0
        and (units * SQUARE) % 128 == 0
    )
    if fits:
        return fused_body(n_dp, n_tensor, *arrays)
    return gathered_body(*arrays)


def solution(mesh):
    in_specs = (
        P("dp", "tensor"),
        P("dp", "tensor"),
        P("dp", "tensor"),
        P(),
        P("tensor", "dp", None),
        P("tensor", "dp", None),
    )
    out_specs = (
        P("dp", "tensor"),
        P("tensor", "dp", None),
        P("tensor", "dp", None),
        P("tensor", "dp", None),
    )
    run = functools.partial(body, mesh.shape["dp"], mesh.shape["tensor"])
    return jax.shard_map(run, mesh=mesh, in_specs=in_specs, out_specs=out_specs, check_vma=False)
```

```python
import functools

import jax
import jax.numpy as jnp
from jax import lax
from jax.experimental import pallas as pl
from jax.experimental.pallas import tpu as pltpu
from jax.sharding import PartitionSpec as P

beta_one = 0.9
beta_two = 0.95
bias_one = 1.0 - 0.9**20
bias_two = 1.0 - 0.95**20
adam_epsilon = 1e-08

MESH = pl.DeviceIdType.MESH
SQUARE = 4
PARTS = 4
LANES = 1024
NT = (((1,), (1,)), ((), ()))
TN = (((0,), (0,)), ((), ()))


def moments(projected, moment_one, moment_two):
    return (
        beta_one * moment_one + (1.0 - beta_one) * projected,
        beta_two * moment_two + (1.0 - beta_two) * projected * projected,
    )


def exchange_kernel(
    line, n_tensor,
    features_in, out_grad, weight, basis_in, moment_one_in, moment_two_in,
    final_tiles, projected_out, step_out,
    features, basis, moment_one, moment_two, tokens, rows, coords, coords_part, tiles, pair_tiles, proj, proj_send, proj_recv,
    local_sem, line_send, line_recv, row_send, row_recv, far_send, far_recv,
    part_send, part_recv, coords_send, coords_recv,
    proj_send_sem, proj_recv_sem, pair_send, pair_recv, final_send, final_recv,
):
    me = lax.axis_index("dp")
    core = lax.axis_index("tensor")
    place = me // SQUARE
    corner = me % SQUARE
    side_x = place * SQUARE + corner + 1 - 2 * (corner % 2)
    side_y = place * SQUARE + corner + 2 - 4 * (corner // 2)
    far = place * SQUARE + (SQUARE - 1 - corner)
    other = 1 - core
    n_tok = out_grad.shape[0]
    width = out_grad.shape[1]
    n_row = weight.shape[0]
    quarter = n_row // 4
    piece = n_tok // PARTS
    own = line // n_tensor

    def on_line(z):
        return z * SQUARE + corner

    def remote(src, dst, send, recv, dp, tensor):
        return pltpu.make_async_remote_copy(
            src_ref=src, dst_ref=dst, send_sem=send, recv_sem=recv,
            device_id=(dp, tensor), device_id_type=MESH,
        )

    def arrived(dst, sem):
        remote(dst, dst, sem, sem, me, other).wait_recv()

    def token_piece(z, p):
        return tokens.at[pl.ds(pl.multiple_of(z * n_tok + p * piece, piece), piece), :]

    keep_tokens = pltpu.make_async_copy(
        out_grad, tokens.at[pl.ds(pl.multiple_of(place * n_tok, n_tok), n_tok), :], local_sem.at[0]
    )
    keep_rows = pltpu.make_async_copy(weight, rows.at[0], local_sem.at[1])
    loads = [
        pltpu.make_async_copy(src, dst, local_sem.at[2 + i])
        for i, (src, dst) in enumerate(
            (
                (features_in, features),
                (basis_in, basis),
                (moment_one_in, moment_one),
                (moment_two_in, moment_two),
            )
        )
    ]
    for load in loads[:2]:
        load.start()
    keep_tokens.start()
    keep_rows.start()
    for load in loads[2:]:
        load.start()

    barrier = pltpu.get_barrier_semaphore()
    greeted = [(me, other), (side_x, core), (side_y, core), (far, core)]
    for s in range(1, line):
        for t in range(n_tensor):
            greeted.append((on_line((place + s) % line), t))
    for dp, t in greeted:
        pl.semaphore_signal(barrier, inc=1, device_id=(dp, t), device_id_type=MESH)
    pl.semaphore_wait(barrier, len(greeted))

    def line_copy(src, z, p, way):
        target = on_line(place + 1 if way == 0 else place - 1)
        return remote(
            src, token_piece(z, p), line_send.at[way, z, p], line_recv.at[z, p], target, core
        )

    def send_own(p):
        for way, there in ((0, place + 1 < line), (1, place > 0)):
            @pl.when(there)
            def _():
                line_copy(out_grad.at[pl.ds(p * piece, piece), :], place, p, way).start()

    for p in range(2):
        send_own(p)

    def row_copy(slot, k):
        return remote(
            weight.at[pl.ds(k * quarter, quarter), :],
            rows.at[slot, pl.ds(k * quarter, quarter), :],
            row_send.at[slot - 1, k], row_recv.at[slot - 1, k],
            side_x if slot == 1 else side_y, core,
        )

    def far_copy(k):
        src = rows.at[1 + k // 2, pl.ds(k * quarter, quarter), :]
        return remote(
            src, rows.at[3, pl.ds(k * quarter, quarter), :], far_send.at[k], far_recv.at[k],
            side_y if k < 2 else side_x, core,
        )

    for slot, k in ((1, 0), (2, 2), (1, 1), (2, 3), (1, 2), (2, 0)):
        row_copy(slot, k).start()

    depth = features.shape[1]
    loads[0].wait()
    loads[1].wait()
    coords_part[0] = jnp.dot(
        features[...],
        basis[pl.ds(pl.multiple_of(core * depth, depth), depth), :],
        preferred_element_type=jnp.float32,
    )
    part_copy = remote(
        coords_part.at[0], coords_part.at[1], part_send.at[0], part_recv.at[0], me, other
    )
    part_copy.start()
    part_copy.wait()
    coords[place] = (coords_part[0] + coords_part[1]).astype(coords.dtype)

    def coords_copy(s):
        z = (place + s) % line
        return remote(
            coords.at[place], coords.at[place], coords_send.at[s], coords_recv.at[place],
            on_line(z), core,
        )

    for s in range(1, line):
        coords_copy(s).start()
    keep_tokens.wait()
    keep_rows.wait()

    strip = SQUARE * projected_out.shape[0]

    def add_projected(z, first=False):
        block = tokens[
            pl.ds(pl.multiple_of(z * n_tok, n_tok), n_tok),
            pl.ds(pl.multiple_of(place * strip, strip), strip),
        ]
        term = lax.dot_general(block, coords[z], TN, preferred_element_type=jnp.float32)
        proj[...] = term if first else proj[...] + term

    def product(first_token, count, slot):
        def step(k, total):
            at = pl.ds(pl.multiple_of(k * LANES, LANES), LANES)
            return total + lax.dot_general(
                tokens[pl.ds(first_token, count), at], rows[slot, :, at], NT,
                preferred_element_type=jnp.float32,
            )

        start = jnp.zeros((count, n_row), jnp.float32)
        return lax.fori_loop(0, width // LANES, step, start)

    def column(slot):
        flip_x = slot % 2
        flip_y = slot // 2
        x, y = corner % 2, corner // 2
        return (x + flip_x) % 2 + 2 * ((y + flip_y) % 2)

    def tile(z, slot):
        got = product(pl.multiple_of(z * n_tok, n_tok), n_tok, slot)
        tiles[z, column(slot)] = got.astype(tiles.dtype)

    def tiles_of(z, slots):
        def one(slot, carry):
            tile(z, slot)
            return carry

        lax.fori_loop(slots[0], slots[1], one, 0)

    add_projected(place, first=True)
    tile(place, 0)

    late = max(line - 2, 1)
    for s in range(1, line):
        from_left = place - s >= 0
        from_right = place + s < line
        for p in range(PARTS):
            for way, here, z, on in (
                (0, from_left, place - s, place + 1 < line),
                (1, from_right, place + s, place > 0),
            ):
                @pl.when(here)
                def _():
                    arrived(token_piece(z, p), line_recv.at[z, p])

                    @pl.when(on)
                    def _():
                        line_copy(token_piece(z, p), z, p, way).start()

            if s == 1 and p + 2 < PARTS:
                send_own(p + 2)

        if s == 1:
            row_copy(1, 3).start()
            row_copy(2, 1).start()
        for here, z in ((from_left, place - s), (from_right, place + s)):
            @pl.when(here)
            def _():
                arrived(coords.at[z], coords_recv.at[z])
                add_projected(z)

        if s == line - 1:
            for r in range(SQUARE):
                proj_send[r] = proj[
                    pl.ds(r * projected_out.shape[0], projected_out.shape[0]), :
                ].astype(proj_send.dtype)
            for r, dp in ((1, side_x), (2, side_y), (3, far)):
                remote(
                    proj_send.at[dp - place * SQUARE], proj_recv.at[r - 1],
                    proj_send_sem.at[r - 1], proj_recv_sem.at[r - 1], dp, core,
                ).start()

        for here, z in ((from_left, place - s), (from_right, place + s)):
            @pl.when(here)
            def _():
                tiles_of(z, (0, 3 if s > late else 1))

        if s == 1:
            for k in (0, 2, 1, 3):
                slot = 1 + k // 2
                arrived(rows.at[slot, pl.ds(k * quarter, quarter), :], row_recv.at[slot - 1, k])
                far_copy(k).start()

        if s == late:
            for slot, k in ((1, 2), (2, 0), (1, 3), (2, 1)):
                arrived(rows.at[slot, pl.ds(k * quarter, quarter), :], row_recv.at[slot - 1, k])

            def early(z, carry):
                @pl.when((z - place <= late) & (place - z <= late))
                def _():
                    tiles_of(z, (1, 3))

                return carry

            lax.fori_loop(0, line, early, 0)

    for k in range(4):
        arrived(rows.at[3, pl.ds(k * quarter, quarter), :], far_recv.at[k])

    def last(t):
        got = product(pl.multiple_of(t * own * n_tok, own * n_tok), own * n_tok, 3)
        for i in range(own):
            tiles[t * own + i, column(3)] = got[i * n_tok : (i + 1) * n_tok].astype(tiles.dtype)

    pair_copies = [
        remote(
            tiles.at[other * own + i], pair_tiles.at[i], pair_send.at[i], pair_recv.at[i], me, other
        )
        for i in range(own)
    ]
    last(other)
    for copy in pair_copies:
        copy.start()
    last(core)

    mine = place // own

    def keep_final(i):
        return pltpu.make_async_copy(
            pair_tiles.at[i], final_tiles.at[place % own], local_sem.at[0]
        )

    for i in range(own):
        pair_copies[i].wait_recv()
        z = core * own + i
        pair_tiles[i] = (
            tiles[z].astype(jnp.float32) + pair_tiles[i].astype(jnp.float32)
        ).astype(pair_tiles.dtype)

        @pl.when(z == place)
        def _():
            keep_final(i).start()

        @pl.when(z != place)
        def _():
            remote(
                pair_tiles.at[i], final_tiles.at[place % own],
                final_send.at[i], final_recv.at[place % own], on_line(z), mine,
            ).start()

    count = projected_out.shape[0]
    total = proj[pl.ds(pl.multiple_of(corner * count, count), count), :]
    for r in range(3):
        arrived(proj_recv.at[r], proj_recv_sem.at[r])
        total = total + proj_recv[r].astype(jnp.float32)
    projected_out[...] = total
    loads[2].wait()
    loads[3].wait()
    one, two = moments(total, moment_one[...], moment_two[...])
    step_out[...] = (
        one / bias_one / (jnp.sqrt(two / bias_two) + adam_epsilon)
    ).astype(step_out.dtype)

    for i in range(own):
        @pl.when(core * own + i != place)
        def _():
            arrived(final_tiles.at[i], final_recv.at[i])

        @pl.when(core * own + i == place)
        def _():
            keep_final(i).wait()

    for s in range(1, line):
        coords_copy(s).wait_send()
    for slot in (1, 2):
        for k in range(4):
            row_copy(slot, k).wait_send()
    for k in range(4):
        far_copy(k).wait_send()
    for s in range(line):
        for p in range(PARTS):
            for way, here, z, on in (
                (0, place - s >= 0, place - s, place + 1 < line),
                (1, place + s < line, place + s, place > 0),
            ):
                @pl.when(here & on)
                def _():
                    line_copy(token_piece(z, p), z, p, way).wait_send()
    for r, dp in ((1, side_x), (2, side_y), (3, far)):
        remote(
            proj_send.at[dp - place * SQUARE], proj_recv.at[r - 1],
            proj_send_sem.at[r - 1], proj_recv_sem.at[r - 1], dp, core,
        ).wait_send()
    for i in range(own):
        pair_copies[i].wait_send()

        @pl.when(core * own + i != place)
        def _():
            remote(
                pair_tiles.at[i], final_tiles.at[place % own],
                final_send.at[i], final_recv.at[place % own], on_line(core * own + i), mine,
            ).wait_send()


def direction_kernel(
    step_dir, projected, moment_one, moment_two, basis, tiles,
    new_one, new_two, direction, feature_grad,
):
    for i in range(tiles.shape[0]):
        feature_grad[:, pl.ds(i * tiles.shape[2], tiles.shape[2])] = tiles[i]
    direction[...] = lax.dot_general(
        step_dir[...], basis[...], NT, preferred_element_type=jnp.float32
    )

    @pl.when(pl.program_id(0) == 1)
    def _():
        new_one[...], new_two[...] = moments(projected[...], moment_one[...], moment_two[...])


def fused_body(n_dp, n_tensor, features, out_grad, weight, basis, moment_one, moment_two):
    line = n_dp // SQUARE
    own = line // n_tensor
    n_tok, width = out_grad.shape
    n_row = weight.shape[0]
    units, rank = moment_one.shape[1:]
    dma = pltpu.SemaphoreType.DMA
    bf16, f32 = jnp.bfloat16, jnp.float32
    tiles, projected, step_dir = pl.pallas_call(
        functools.partial(exchange_kernel, line, n_tensor),
        out_shape=(
            jax.ShapeDtypeStruct((own, SQUARE, n_tok, n_row), bf16),
            jax.ShapeDtypeStruct((units, rank), f32),
            jax.ShapeDtypeStruct((units, rank), bf16),
        ),
        in_specs=[pl.BlockSpec(memory_space=pltpu.HBM)] * 6,
        out_specs=[
            pl.BlockSpec(memory_space=pl.ANY),
            pl.BlockSpec(memory_space=pltpu.VMEM),
            pl.BlockSpec(memory_space=pltpu.VMEM),
        ],
        scratch_shapes=[
            pltpu.VMEM(features.shape, bf16),
            pltpu.VMEM(basis.shape, bf16),
            pltpu.VMEM((units, rank), f32),
            pltpu.VMEM((units, rank), f32),
            pltpu.VMEM((line * n_tok, width), bf16),
            pltpu.VMEM((SQUARE, n_row, width), bf16),
            pltpu.VMEM((line, n_tok, rank), bf16),
            pltpu.VMEM((2, n_tok, rank), f32),
            pltpu.VMEM((line, SQUARE, n_tok, n_row), bf16),
            pltpu.VMEM((own, SQUARE, n_tok, n_row), bf16),
            pltpu.VMEM((SQUARE * units, rank), f32),
            pltpu.VMEM((SQUARE, units, rank), bf16),
            pltpu.VMEM((SQUARE - 1, units, rank), bf16),
            dma((6,)),
            dma((2, line, PARTS)),
            dma((line, PARTS)),
            dma((2, 4)),
            dma((2, 4)),
            dma((4,)),
            dma((4,)),
            dma((1,)),
            dma((1,)),
            dma((line,)),
            dma((line,)),
            dma((SQUARE - 1,)),
            dma((SQUARE - 1,)),
            dma((own,)),
            dma((own,)),
            dma((own,)),
            dma((own,)),
        ],
        compiler_params=pltpu.CompilerParams(
            collective_id=0, has_side_effects=True, vmem_limit_bytes=64 << 20
        ),
        name="exchange",
    )(features, out_grad, weight, basis, moment_one[0], moment_two[0])

    n_feature = basis.shape[0]
    block = n_feature // 4
    whole = pl.BlockSpec((units, rank), lambda i: (0, 0))
    count = own * SQUARE // 4
    new_one, new_two, direction, feature_grad = pl.pallas_call(
        direction_kernel,
        grid=(n_feature // block,),
        out_shape=(
            jax.ShapeDtypeStruct((units, rank), f32),
            jax.ShapeDtypeStruct((units, rank), f32),
            jax.ShapeDtypeStruct((units, n_feature), f32),
            jax.ShapeDtypeStruct(features.shape, bf16),
        ),
        in_specs=[
            whole, whole, whole, whole,
            pl.BlockSpec((block, rank), lambda i: (i, 0)),
            pl.BlockSpec((count, n_tok, n_row), lambda i: (i, 0, 0)),
        ],
        out_specs=[
            whole, whole,
            pl.BlockSpec((units, block), lambda i: (0, i)),
            pl.BlockSpec((n_tok, count * n_row), lambda i: (0, i)),
        ],
        compiler_params=pltpu.CompilerParams(vmem_limit_bytes=64 << 20),
        name="direction",
    )(step_dir, projected, moment_one[0], moment_two[0], basis, tiles.reshape(own * SQUARE, n_tok, n_row))
    return (feature_grad, new_one[None], new_two[None], direction[None])


def gathered_body(features, out_grad, weight, basis, moment_one, moment_two):
    partial_value = jnp.einsum(
        "tf,df->td",
        out_grad,
        lax.all_gather(weight, "dp", axis=0, tiled=True),
        preferred_element_type=jnp.float32,
    )
    feature_grad = lax.psum_scatter(
        partial_value.astype(jnp.bfloat16), "tensor", scatter_dimension=1, tiled=True
    )
    part_width = features.shape[1]
    basis_part = lax.dynamic_slice_in_dim(
        basis, lax.axis_index("tensor") * part_width, part_width, 0
    )
    local_coords = jnp.dot(features, basis_part, preferred_element_type=jnp.float32)
    coords = lax.psum(local_coords, "tensor")
    coords = coords.astype(jnp.bfloat16)
    projected = lax.psum_scatter(
        jnp.einsum("tf,tr->fr", out_grad, coords, preferred_element_type=jnp.float32),
        "dp",
        scatter_dimension=0,
        tiled=True,
    )
    first = moment_one[0]
    second = moment_two[0]
    new_one = beta_one * first + (1.0 - beta_one) * projected
    new_two = beta_two * second + (1.0 - beta_two) * projected * projected
    step_dir = (new_one / bias_one / (jnp.sqrt(new_two / bias_two) + adam_epsilon)).astype(
        jnp.bfloat16
    )
    direction = jnp.einsum("cr,dr->cd", step_dir, basis, preferred_element_type=jnp.float32)
    return (feature_grad, new_one[None], new_two[None], direction[None])


def body(n_dp, n_tensor, *arrays):
    _, out_grad, weight, basis, moment_one, _ = arrays
    line = n_dp // SQUARE
    units = moment_one.shape[1]
    fits = (
        n_tensor == 2
        and n_dp % SQUARE == 0
        and line % n_tensor == 0
        and out_grad.shape[1] % LANES == 0
        and out_grad.shape[0] % (16 * PARTS) == 0
        and weight.shape[0] % 128 == 0
        and units % 16 == 0
        and basis.shape[0] % 512 == 0
        and (units * SQUARE) % 128 == 0
    )
    if fits:
        return fused_body(n_dp, n_tensor, *arrays)
    return gathered_body(*arrays)


def solution(mesh):
    in_specs = (
        P("dp", "tensor"),
        P("dp", "tensor"),
        P("dp", "tensor"),
        P(),
        P("tensor", "dp", None),
        P("tensor", "dp", None),
    )
    out_specs = (
        P("dp", "tensor"),
        P("tensor", "dp", None),
        P("tensor", "dp", None),
        P("tensor", "dp", None),
    )
    run = functools.partial(body, mesh.shape["dp"], mesh.shape["tensor"])
    return jax.shard_map(run, mesh=mesh, in_specs=in_specs, out_specs=out_specs, check_vma=False)
```

```python
import functools

import jax
import jax.numpy as jnp
from jax import lax
from jax.experimental import pallas as pl
from jax.experimental.pallas import tpu as pltpu
from jax.sharding import PartitionSpec as P

beta_one = 0.9
beta_two = 0.95
bias_one = 1.0 - 0.9**20
bias_two = 1.0 - 0.95**20
adam_epsilon = 1e-08

MESH = pl.DeviceIdType.MESH
SQUARE = 4
PARTS = 4
NT = (((1,), (1,)), ((), ()))
TN = (((0,), (0,)), ((), ()))


def moments(projected, moment_one, moment_two):
    return (
        beta_one * moment_one + (1.0 - beta_one) * projected,
        beta_two * moment_two + (1.0 - beta_two) * projected * projected,
    )


def exchange_kernel(
    line, n_tensor,
    features_in, out_grad, weight, basis_in, moment_one_in, moment_two_in,
    final_tiles, projected_out, step_out,
    features, basis, moment_one, moment_two, tokens, rows, coords, coords_part, tiles, pair_tiles, proj, proj_send, proj_recv,
    local_sem, line_send, line_recv, row_send, row_recv, far_send, far_recv,
    part_send, part_recv, coords_send, coords_recv,
    proj_send_sem, proj_recv_sem, pair_send, pair_recv, final_send, final_recv, keep_sem,
):
    me = lax.axis_index("dp")
    core = lax.axis_index("tensor")
    place = me // SQUARE
    corner = me % SQUARE
    side_x = place * SQUARE + corner + 1 - 2 * (corner % 2)
    side_y = place * SQUARE + corner + 2 - 4 * (corner // 2)
    far = place * SQUARE + (SQUARE - 1 - corner)
    other = 1 - core
    n_tok = out_grad.shape[0]
    width = out_grad.shape[1]
    n_row = weight.shape[0]
    quarter = n_row // 4
    piece = n_tok // PARTS
    own = line // n_tensor

    def on_line(z):
        return z * SQUARE + corner

    def remote(src, dst, send, recv, dp, tensor):
        return pltpu.make_async_remote_copy(
            src_ref=src, dst_ref=dst, send_sem=send, recv_sem=recv,
            device_id=(dp, tensor), device_id_type=MESH,
        )

    def arrived(dst, sem):
        remote(dst, dst, sem, sem, me, other).wait_recv()

    def token_piece(z, p):
        return tokens.at[pl.ds(pl.multiple_of(z * n_tok + p * piece, piece), piece), :]

    keep_tokens = pltpu.make_async_copy(
        out_grad, tokens.at[pl.ds(pl.multiple_of(place * n_tok, n_tok), n_tok), :], local_sem.at[0]
    )
    keep_rows = pltpu.make_async_copy(weight, rows.at[0], local_sem.at[1])
    loads = [
        pltpu.make_async_copy(src, dst, local_sem.at[2 + i])
        for i, (src, dst) in enumerate(
            (
                (features_in, features),
                (basis_in, basis),
                (moment_one_in, moment_one),
                (moment_two_in, moment_two),
            )
        )
    ]
    for load in loads[:2]:
        load.start()
    keep_tokens.start()
    keep_rows.start()
    for load in loads[2:]:
        load.start()

    barrier = pltpu.get_barrier_semaphore()
    greeted = [(me, other), (side_x, core), (side_y, core), (far, core)]
    for s in range(1, line):
        for t in range(n_tensor):
            greeted.append((on_line((place + s) % line), t))
    for dp, t in greeted:
        pl.semaphore_signal(barrier, inc=1, device_id=(dp, t), device_id_type=MESH)
    pl.semaphore_wait(barrier, len(greeted))

    def line_copy(src, z, p, way):
        target = on_line(place + 1 if way == 0 else place - 1)
        return remote(
            src, token_piece(z, p), line_send.at[way, z, p], line_recv.at[z, p], target, core
        )

    def send_own(p):
        for way, there in ((0, place + 1 < line), (1, place > 0)):
            @pl.when(there)
            def _():
                line_copy(out_grad.at[pl.ds(p * piece, piece), :], place, p, way).start()

    for p in range(2):
        send_own(p)

    def row_copy(slot, k):
        return remote(
            weight.at[pl.ds(k * quarter, quarter), :],
            rows.at[slot, pl.ds(k * quarter, quarter), :],
            row_send.at[slot - 1, k], row_recv.at[slot - 1, k],
            side_x if slot == 1 else side_y, core,
        )

    def far_copy(k):
        src = rows.at[1 + k // 2, pl.ds(k * quarter, quarter), :]
        return remote(
            src, rows.at[3, pl.ds(k * quarter, quarter), :], far_send.at[k], far_recv.at[k],
            side_y if k < 2 else side_x, core,
        )

    for slot, k in ((1, 0), (2, 2), (1, 1), (2, 3), (1, 2), (2, 0)):
        row_copy(slot, k).start()

    depth = features.shape[1]
    loads[0].wait()
    loads[1].wait()
    coords_part[0] = jnp.dot(
        features[...],
        basis[pl.ds(pl.multiple_of(core * depth, depth), depth), :],
        preferred_element_type=jnp.float32,
    )
    part_copy = remote(
        coords_part.at[0], coords_part.at[1], part_send.at[0], part_recv.at[0], me, other
    )
    part_copy.start()
    part_copy.wait()
    coords[place] = (coords_part[0] + coords_part[1]).astype(coords.dtype)

    def coords_copy(s):
        z = (place + s) % line
        return remote(
            coords.at[place], coords.at[place], coords_send.at[s], coords_recv.at[place],
            on_line(z), core,
        )

    for s in range(1, line):
        coords_copy(s).start()
    keep_tokens.wait()
    keep_rows.wait()

    strip = SQUARE * projected_out.shape[0]

    def add_projected(z, first=False):
        block = tokens[
            pl.ds(pl.multiple_of(z * n_tok, n_tok), n_tok),
            pl.ds(pl.multiple_of(place * strip, strip), strip),
        ]
        term = lax.dot_general(block, coords[z], TN, preferred_element_type=jnp.float32)
        proj[...] = term if first else proj[...] + term

    def product(first_token, count, slot):
        return lax.dot_general(
            tokens[pl.ds(first_token, count), :], rows[slot], NT,
            preferred_element_type=jnp.float32,
        )

    def column(slot):
        flip_x = slot % 2
        flip_y = slot // 2
        x, y = corner % 2, corner // 2
        return (x + flip_x) % 2 + 2 * ((y + flip_y) % 2)

    def tile(z, slot):
        got = product(pl.multiple_of(z * n_tok, n_tok), n_tok, slot)
        tiles[z, column(slot)] = got.astype(tiles.dtype)

    def tiles_of(z, slots):
        def one(slot, carry):
            tile(z, slot)
            return carry

        lax.fori_loop(slots[0], slots[1], one, 0)

    add_projected(place, first=True)
    tile(place, 0)

    late = max(line - 2, 1)
    for s in range(1, line):
        from_left = place - s >= 0
        from_right = place + s < line
        for p in range(PARTS):
            for way, here, z, on in (
                (0, from_left, place - s, place + 1 < line),
                (1, from_right, place + s, place > 0),
            ):
                @pl.when(here)
                def _():
                    arrived(token_piece(z, p), line_recv.at[z, p])

                    @pl.when(on)
                    def _():
                        line_copy(token_piece(z, p), z, p, way).start()

            if s == 1 and p + 2 < PARTS:
                send_own(p + 2)

        if s == 1:
            row_copy(1, 3).start()
            row_copy(2, 1).start()
        for here, z in ((from_left, place - s), (from_right, place + s)):
            @pl.when(here)
            def _():
                arrived(coords.at[z], coords_recv.at[z])
                add_projected(z)

        if s == line - 1:
            for r in range(SQUARE):
                proj_send[r] = proj[
                    pl.ds(r * projected_out.shape[0], projected_out.shape[0]), :
                ].astype(proj_send.dtype)
            for r, dp in ((1, side_x), (2, side_y), (3, far)):
                remote(
                    proj_send.at[dp - place * SQUARE], proj_recv.at[r - 1],
                    proj_send_sem.at[r - 1], proj_recv_sem.at[r - 1], dp, core,
                ).start()

        for here, z in ((from_left, place - s), (from_right, place + s)):
            @pl.when(here)
            def _():
                tiles_of(z, (0, 3 if s > late else 1))

        if s == 1:
            for k in (0, 2, 1, 3):
                slot = 1 + k // 2
                arrived(rows.at[slot, pl.ds(k * quarter, quarter), :], row_recv.at[slot - 1, k])
                far_copy(k).start()

        if s == late:
            for slot, k in ((1, 2), (2, 0), (1, 3), (2, 1)):
                arrived(rows.at[slot, pl.ds(k * quarter, quarter), :], row_recv.at[slot - 1, k])

            def early(z, carry):
                @pl.when((z - place <= late) & (place - z <= late))
                def _():
                    tiles_of(z, (1, 3))

                return carry

            lax.fori_loop(0, line, early, 0)

    mine = place // own

    def pair_copy(i, slot):
        c = column(slot)
        return remote(
            tiles.at[other * own + i, c], pair_tiles.at[i, c],
            pair_send.at[i, slot], pair_recv.at[i, slot], me, other,
        )

    def final_copy(i, slot):
        c = column(slot)
        return remote(
            pair_tiles.at[i, c], final_tiles.at[place % own, c],
            final_send.at[i, slot], final_recv.at[place % own, slot],
            on_line(core * own + i), mine,
        )

    def keep_final(i, slot):
        c = column(slot)
        return pltpu.make_async_copy(
            pair_tiles.at[i, c], final_tiles.at[place % own, c], keep_sem.at[slot]
        )

    def finish(slot):
        c = column(slot)
        for i in range(own):
            pair_copy(i, slot).wait_recv()
            z = core * own + i
            pair_tiles[i, c] = (
                tiles[z, c].astype(jnp.float32) + pair_tiles[i, c].astype(jnp.float32)
            ).astype(pair_tiles.dtype)

            @pl.when(z == place)
            def _():
                keep_final(i, slot).start()

            @pl.when(z != place)
            def _():
                final_copy(i, slot).start()

    for slot in range(SQUARE - 1):
        for i in range(own):
            pair_copy(i, slot).start()
    for slot in range(SQUARE - 1):
        finish(slot)

    for k in range(4):
        arrived(rows.at[3, pl.ds(k * quarter, quarter), :], far_recv.at[k])

    def last(t):
        got = product(pl.multiple_of(t * own * n_tok, own * n_tok), own * n_tok, 3)
        for i in range(own):
            tiles[t * own + i, column(3)] = got[i * n_tok : (i + 1) * n_tok].astype(tiles.dtype)

    last(other)
    for i in range(own):
        pair_copy(i, 3).start()
    last(core)
    finish(3)

    count = projected_out.shape[0]
    total = proj[pl.ds(pl.multiple_of(corner * count, count), count), :]
    for r in range(3):
        arrived(proj_recv.at[r], proj_recv_sem.at[r])
        total = total + proj_recv[r].astype(jnp.float32)
    projected_out[...] = total
    loads[2].wait()
    loads[3].wait()
    one, two = moments(total, moment_one[...], moment_two[...])
    step_out[...] = (
        one / bias_one / (jnp.sqrt(two / bias_two) + adam_epsilon)
    ).astype(step_out.dtype)

    for i in range(own):
        for slot in range(SQUARE):
            @pl.when(core * own + i != place)
            def _():
                arrived(final_tiles.at[i, column(slot)], final_recv.at[i, slot])

            @pl.when(core * own + i == place)
            def _():
                keep_final(i, slot).wait()

    for s in range(1, line):
        coords_copy(s).wait_send()
    for slot in (1, 2):
        for k in range(4):
            row_copy(slot, k).wait_send()
    for k in range(4):
        far_copy(k).wait_send()
    for s in range(line):
        for p in range(PARTS):
            for way, here, z, on in (
                (0, place - s >= 0, place - s, place + 1 < line),
                (1, place + s < line, place + s, place > 0),
            ):
                @pl.when(here & on)
                def _():
                    line_copy(token_piece(z, p), z, p, way).wait_send()
    for r, dp in ((1, side_x), (2, side_y), (3, far)):
        remote(
            proj_send.at[dp - place * SQUARE], proj_recv.at[r - 1],
            proj_send_sem.at[r - 1], proj_recv_sem.at[r - 1], dp, core,
        ).wait_send()
    for i in range(own):
        for slot in range(SQUARE):
            pair_copy(i, slot).wait_send()

            @pl.when(core * own + i != place)
            def _():
                final_copy(i, slot).wait_send()


def direction_kernel(
    step_dir, projected, moment_one, moment_two, basis, tiles,
    new_one, new_two, direction, feature_grad,
):
    for i in range(tiles.shape[0]):
        feature_grad[:, pl.ds(i * tiles.shape[2], tiles.shape[2])] = tiles[i]
    direction[...] = lax.dot_general(
        step_dir[...], basis[...], NT, preferred_element_type=jnp.float32
    )

    @pl.when(pl.program_id(0) == 1)
    def _():
        new_one[...], new_two[...] = moments(projected[...], moment_one[...], moment_two[...])


def fused_body(n_dp, n_tensor, features, out_grad, weight, basis, moment_one, moment_two):
    line = n_dp // SQUARE
    own = line // n_tensor
    n_tok, width = out_grad.shape
    n_row = weight.shape[0]
    units, rank = moment_one.shape[1:]
    dma = pltpu.SemaphoreType.DMA
    bf16, f32 = jnp.bfloat16, jnp.float32
    tiles, projected, step_dir = pl.pallas_call(
        functools.partial(exchange_kernel, line, n_tensor),
        out_shape=(
            jax.ShapeDtypeStruct((own, SQUARE, n_tok, n_row), bf16),
            jax.ShapeDtypeStruct((units, rank), f32),
            jax.ShapeDtypeStruct((units, rank), bf16),
        ),
        in_specs=[pl.BlockSpec(memory_space=pltpu.HBM)] * 6,
        out_specs=[
            pl.BlockSpec(memory_space=pl.ANY),
            pl.BlockSpec(memory_space=pltpu.VMEM),
            pl.BlockSpec(memory_space=pltpu.VMEM),
        ],
        scratch_shapes=[
            pltpu.VMEM(features.shape, bf16),
            pltpu.VMEM(basis.shape, bf16),
            pltpu.VMEM((units, rank), f32),
            pltpu.VMEM((units, rank), f32),
            pltpu.VMEM((line * n_tok, width), bf16),
            pltpu.VMEM((SQUARE, n_row, width), bf16),
            pltpu.VMEM((line, n_tok, rank), bf16),
            pltpu.VMEM((2, n_tok, rank), f32),
            pltpu.VMEM((line, SQUARE, n_tok, n_row), bf16),
            pltpu.VMEM((own, SQUARE, n_tok, n_row), bf16),
            pltpu.VMEM((SQUARE * units, rank), f32),
            pltpu.VMEM((SQUARE, units, rank), bf16),
            pltpu.VMEM((SQUARE - 1, units, rank), bf16),
            dma((6,)),
            dma((2, line, PARTS)),
            dma((line, PARTS)),
            dma((2, 4)),
            dma((2, 4)),
            dma((4,)),
            dma((4,)),
            dma((1,)),
            dma((1,)),
            dma((line,)),
            dma((line,)),
            dma((SQUARE - 1,)),
            dma((SQUARE - 1,)),
            dma((own, SQUARE)),
            dma((own, SQUARE)),
            dma((own, SQUARE)),
            dma((own, SQUARE)),
            dma((SQUARE,)),
        ],
        compiler_params=pltpu.CompilerParams(
            collective_id=0, has_side_effects=True, vmem_limit_bytes=64 << 20
        ),
        name="exchange",
    )(features, out_grad, weight, basis, moment_one[0], moment_two[0])

    n_feature = basis.shape[0]
    block = n_feature // 4
    whole = pl.BlockSpec((units, rank), lambda i: (0, 0))
    count = own * SQUARE // 4
    new_one, new_two, direction, feature_grad = pl.pallas_call(
        direction_kernel,
        grid=(n_feature // block,),
        out_shape=(
            jax.ShapeDtypeStruct((units, rank), f32),
            jax.ShapeDtypeStruct((units, rank), f32),
            jax.ShapeDtypeStruct((units, n_feature), f32),
            jax.ShapeDtypeStruct(features.shape, bf16),
        ),
        in_specs=[
            whole, whole, whole, whole,
            pl.BlockSpec((block, rank), lambda i: (i, 0)),
            pl.BlockSpec((count, n_tok, n_row), lambda i: (i, 0, 0)),
        ],
        out_specs=[
            whole, whole,
            pl.BlockSpec((units, block), lambda i: (0, i)),
            pl.BlockSpec((n_tok, count * n_row), lambda i: (0, i)),
        ],
        compiler_params=pltpu.CompilerParams(vmem_limit_bytes=64 << 20),
        name="direction",
    )(step_dir, projected, moment_one[0], moment_two[0], basis, tiles.reshape(own * SQUARE, n_tok, n_row))
    return (feature_grad, new_one[None], new_two[None], direction[None])


def gathered_body(features, out_grad, weight, basis, moment_one, moment_two):
    partial_value = jnp.einsum(
        "tf,df->td",
        out_grad,
        lax.all_gather(weight, "dp", axis=0, tiled=True),
        preferred_element_type=jnp.float32,
    )
    feature_grad = lax.psum_scatter(
        partial_value.astype(jnp.bfloat16), "tensor", scatter_dimension=1, tiled=True
    )
    part_width = features.shape[1]
    basis_part = lax.dynamic_slice_in_dim(
        basis, lax.axis_index("tensor") * part_width, part_width, 0
    )
    local_coords = jnp.dot(features, basis_part, preferred_element_type=jnp.float32)
    coords = lax.psum(local_coords, "tensor")
    coords = coords.astype(jnp.bfloat16)
    projected = lax.psum_scatter(
        jnp.einsum("tf,tr->fr", out_grad, coords, preferred_element_type=jnp.float32),
        "dp",
        scatter_dimension=0,
        tiled=True,
    )
    first = moment_one[0]
    second = moment_two[0]
    new_one = beta_one * first + (1.0 - beta_one) * projected
    new_two = beta_two * second + (1.0 - beta_two) * projected * projected
    step_dir = (new_one / bias_one / (jnp.sqrt(new_two / bias_two) + adam_epsilon)).astype(
        jnp.bfloat16
    )
    direction = jnp.einsum("cr,dr->cd", step_dir, basis, preferred_element_type=jnp.float32)
    return (feature_grad, new_one[None], new_two[None], direction[None])


def body(n_dp, n_tensor, *arrays):
    _, out_grad, weight, basis, moment_one, _ = arrays
    line = n_dp // SQUARE
    units = moment_one.shape[1]
    fits = (
        n_tensor == 2
        and n_dp % SQUARE == 0
        and line % n_tensor == 0
        and out_grad.shape[1] % 256 == 0
        and out_grad.shape[0] % (16 * PARTS) == 0
        and weight.shape[0] % 128 == 0
        and units % 16 == 0
        and basis.shape[0] % 512 == 0
        and (units * SQUARE) % 128 == 0
    )
    if fits:
        return fused_body(n_dp, n_tensor, *arrays)
    return gathered_body(*arrays)


def solution(mesh):
    in_specs = (
        P("dp", "tensor"),
        P("dp", "tensor"),
        P("dp", "tensor"),
        P(),
        P("tensor", "dp", None),
        P("tensor", "dp", None),
    )
    out_specs = (
        P("dp", "tensor"),
        P("tensor", "dp", None),
        P("tensor", "dp", None),
        P("tensor", "dp", None),
    )
    run = functools.partial(body, mesh.shape["dp"], mesh.shape["tensor"])
    return jax.shard_map(run, mesh=mesh, in_specs=in_specs, out_specs=out_specs, check_vma=False)
```

```python
import functools

import jax
import jax.numpy as jnp
from jax import lax
from jax.experimental import pallas as pl
from jax.experimental.pallas import tpu as pltpu
from jax.sharding import PartitionSpec as P

beta_one = 0.9
beta_two = 0.95
bias_one = 1.0 - 0.9**20
bias_two = 1.0 - 0.95**20
adam_epsilon = 1e-08

MESH = pl.DeviceIdType.MESH
SQUARE = 4
PARTS = 4
NT = (((1,), (1,)), ((), ()))
TN = (((0,), (0,)), ((), ()))


def moments(projected, moment_one, moment_two):
    return (
        beta_one * moment_one + (1.0 - beta_one) * projected,
        beta_two * moment_two + (1.0 - beta_two) * projected * projected,
    )


def exchange_kernel(
    line, n_tensor,
    features_in, out_grad, weight, basis_in, moment_one_in, moment_two_in,
    final_tiles, projected_out, step_out,
    features, basis, moment_one, moment_two, tokens, rows, coords, coords_part, tiles, pair_tiles, proj, proj_send, proj_recv,
    local_sem, line_send, line_recv, row_send, row_recv, far_send, far_recv,
    part_send, part_recv, coords_send, coords_recv,
    proj_send_sem, proj_recv_sem, pair_send, pair_recv, final_send, final_recv, keep_sem,
):
    me = lax.axis_index("dp")
    core = lax.axis_index("tensor")
    place = me // SQUARE
    corner = me % SQUARE
    side_x = place * SQUARE + corner + 1 - 2 * (corner % 2)
    side_y = place * SQUARE + corner + 2 - 4 * (corner // 2)
    far = place * SQUARE + (SQUARE - 1 - corner)
    other = 1 - core
    n_tok = out_grad.shape[0]
    width = out_grad.shape[1]
    n_row = weight.shape[0]
    quarter = n_row // 4
    piece = n_tok // PARTS
    own = line // n_tensor

    def on_line(z):
        return z * SQUARE + corner

    def remote(src, dst, send, recv, dp, tensor):
        return pltpu.make_async_remote_copy(
            src_ref=src, dst_ref=dst, send_sem=send, recv_sem=recv,
            device_id=(dp, tensor), device_id_type=MESH,
        )

    def arrived(dst, sem):
        remote(dst, dst, sem, sem, me, other).wait_recv()

    def token_piece(z, p):
        return tokens.at[pl.ds(pl.multiple_of(z * n_tok + p * piece, piece), piece), :]

    keep_tokens = pltpu.make_async_copy(
        out_grad, tokens.at[pl.ds(pl.multiple_of(place * n_tok, n_tok), n_tok), :], local_sem.at[0]
    )
    keep_rows = pltpu.make_async_copy(weight, rows.at[0], local_sem.at[1])
    loads = [
        pltpu.make_async_copy(src, dst, local_sem.at[2 + i])
        for i, (src, dst) in enumerate(
            (
                (features_in, features),
                (basis_in, basis),
                (moment_one_in, moment_one),
                (moment_two_in, moment_two),
            )
        )
    ]
    for load in loads[:2]:
        load.start()
    keep_tokens.start()
    keep_rows.start()
    for load in loads[2:]:
        load.start()

    barrier = pltpu.get_barrier_semaphore()
    greeted = [(me, other), (side_x, core), (side_y, core), (far, core)]
    for s in range(1, line):
        for t in range(n_tensor):
            greeted.append((on_line((place + s) % line), t))
    for dp, t in greeted:
        pl.semaphore_signal(barrier, inc=1, device_id=(dp, t), device_id_type=MESH)
    pl.semaphore_wait(barrier, len(greeted))

    def line_copy(src, z, p, way):
        target = on_line(place + 1 if way == 0 else place - 1)
        return remote(
            src, token_piece(z, p), line_send.at[way, z, p], line_recv.at[z, p], target, core
        )

    def send_own(p):
        for way, there in ((0, place + 1 < line), (1, place > 0)):
            @pl.when(there)
            def _():
                line_copy(out_grad.at[pl.ds(p * piece, piece), :], place, p, way).start()

    for p in range(2):
        send_own(p)

    def row_copy(slot, k):
        return remote(
            weight.at[pl.ds(k * quarter, quarter), :],
            rows.at[slot, pl.ds(k * quarter, quarter), :],
            row_send.at[slot - 1, k], row_recv.at[slot - 1, k],
            side_x if slot == 1 else side_y, core,
        )

    def far_copy(k):
        src = rows.at[1 + k // 2, pl.ds(k * quarter, quarter), :]
        return remote(
            src, rows.at[3, pl.ds(k * quarter, quarter), :], far_send.at[k], far_recv.at[k],
            side_y if k < 2 else side_x, core,
        )

    for slot, k in ((1, 0), (2, 2), (1, 1), (2, 3), (1, 2), (2, 0)):
        row_copy(slot, k).start()

    depth = features.shape[1]
    loads[0].wait()
    loads[1].wait()
    coords_part[0] = jnp.dot(
        features[...],
        basis[pl.ds(pl.multiple_of(core * depth, depth), depth), :],
        preferred_element_type=jnp.float32,
    )
    part_copy = remote(
        coords_part.at[0], coords_part.at[1], part_send.at[0], part_recv.at[0], me, other
    )
    part_copy.start()
    part_copy.wait()
    coords[place] = (coords_part[0] + coords_part[1]).astype(coords.dtype)

    def coords_copy(s):
        z = (place + s) % line
        return remote(
            coords.at[place], coords.at[place], coords_send.at[s], coords_recv.at[place],
            on_line(z), core,
        )

    for s in range(1, line):
        coords_copy(s).start()
    keep_tokens.wait()
    keep_rows.wait()

    strip = SQUARE * projected_out.shape[0]

    def add_projected(z, first=False):
        block = tokens[
            pl.ds(pl.multiple_of(z * n_tok, n_tok), n_tok),
            pl.ds(pl.multiple_of(place * strip, strip), strip),
        ]
        term = lax.dot_general(block, coords[z], TN, preferred_element_type=jnp.float32)
        proj[...] = term if first else proj[...] + term

    def product(first_token, count, slot):
        return lax.dot_general(
            tokens[pl.ds(first_token, count), :], rows[slot], NT,
            preferred_element_type=jnp.float32,
        )

    def column(slot):
        flip_x = slot % 2
        flip_y = slot // 2
        x, y = corner % 2, corner // 2
        return (x + flip_x) % 2 + 2 * ((y + flip_y) % 2)

    def tile(z, slot):
        got = product(pl.multiple_of(z * n_tok, n_tok), n_tok, slot)
        tiles[z, column(slot)] = got.astype(tiles.dtype)

    def tiles_of(z, slots):
        def one(slot, carry):
            tile(z, slot)
            return carry

        lax.fori_loop(slots[0], slots[1], one, 0)

    def far_tiles(z):
        block = tokens[pl.ds(pl.multiple_of(z * n_tok, n_tok), n_tok), :]
        got = lax.dot_general(
            block, rows[0:3].reshape(3 * n_row, width), NT, preferred_element_type=jnp.float32
        )
        for slot in range(3):
            tiles[z, column(slot)] = got[:, slot * n_row : (slot + 1) * n_row].astype(tiles.dtype)

    add_projected(place, first=True)
    tile(place, 0)

    late = max(line - 2, 1)
    mine = place // own

    def pair_copy(i, slot):
        c = column(slot)
        return remote(
            tiles.at[other * own + i, c], pair_tiles.at[i, c],
            pair_send.at[i, slot], pair_recv.at[i, slot], me, other,
        )

    def final_copy(i, slot):
        c = column(slot)
        return remote(
            pair_tiles.at[i, c], final_tiles.at[place % own, c],
            final_send.at[i, slot], final_recv.at[place % own, slot],
            on_line(core * own + i), mine,
        )

    def keep_final(i, slot):
        c = column(slot)
        return pltpu.make_async_copy(
            pair_tiles.at[i, c], final_tiles.at[place % own, c], keep_sem.at[slot]
        )

    def near(z):
        return (z - place <= late) & (place - z <= late)

    def finish(i, slot):
        c = column(slot)
        pair_copy(i, slot).wait_recv()
        z = core * own + i
        pair_tiles[i, c] = (
            tiles[z, c].astype(jnp.float32) + pair_tiles[i, c].astype(jnp.float32)
        ).astype(pair_tiles.dtype)

        @pl.when(z == place)
        def _():
            keep_final(i, slot).start()

        @pl.when(z != place)
        def _():
            final_copy(i, slot).start()

    def early_slots(now):
        for i in range(own):
            @pl.when(near(other * own + i) == now)
            def _():
                for slot in range(SQUARE - 1):
                    pair_copy(i, slot).start()

        for i in range(own):
            @pl.when(near(core * own + i) == now)
            def _():
                for slot in range(SQUARE - 1):
                    finish(i, slot)

    for s in range(1, line):
        from_left = place - s >= 0
        from_right = place + s < line
        for p in range(PARTS):
            for way, here, z, on in (
                (0, from_left, place - s, place + 1 < line),
                (1, from_right, place + s, place > 0),
            ):
                @pl.when(here)
                def _():
                    arrived(token_piece(z, p), line_recv.at[z, p])

                    @pl.when(on)
                    def _():
                        line_copy(token_piece(z, p), z, p, way).start()

            if s == 1 and p + 2 < PARTS:
                send_own(p + 2)

        if s == 1:
            row_copy(1, 3).start()
            row_copy(2, 1).start()
        for here, z in ((from_left, place - s), (from_right, place + s)):
            @pl.when(here)
            def _():
                arrived(coords.at[z], coords_recv.at[z])
                add_projected(z)

        if s == line - 1:
            for r in range(SQUARE):
                proj_send[r] = proj[
                    pl.ds(r * projected_out.shape[0], projected_out.shape[0]), :
                ].astype(proj_send.dtype)
            for r, dp in ((1, side_x), (2, side_y), (3, far)):
                remote(
                    proj_send.at[dp - place * SQUARE], proj_recv.at[r - 1],
                    proj_send_sem.at[r - 1], proj_recv_sem.at[r - 1], dp, core,
                ).start()

        for here, z in ((from_left, place - s), (from_right, place + s)):
            @pl.when(here)
            def _():
                if s > late:
                    far_tiles(z)
                else:
                    tile(z, 0)

        if s == 1:
            for k in (0, 2, 1, 3):
                slot = 1 + k // 2
                arrived(rows.at[slot, pl.ds(k * quarter, quarter), :], row_recv.at[slot - 1, k])
                far_copy(k).start()

        if s == late:
            for slot, k in ((1, 2), (2, 0), (1, 3), (2, 1)):
                arrived(rows.at[slot, pl.ds(k * quarter, quarter), :], row_recv.at[slot - 1, k])

            def early(z, carry):
                @pl.when(near(z))
                def _():
                    tiles_of(z, (1, 3))

                return carry

            lax.fori_loop(0, line, early, 0)
            early_slots(True)

    early_slots(False)

    for k in range(4):
        arrived(rows.at[3, pl.ds(k * quarter, quarter), :], far_recv.at[k])

    def last(t):
        got = product(pl.multiple_of(t * own * n_tok, own * n_tok), own * n_tok, 3)
        for i in range(own):
            tiles[t * own + i, column(3)] = got[i * n_tok : (i + 1) * n_tok].astype(tiles.dtype)

    last(other)
    for i in range(own):
        pair_copy(i, 3).start()
    last(core)
    for i in range(own):
        finish(i, 3)

    count = projected_out.shape[0]
    total = proj[pl.ds(pl.multiple_of(corner * count, count), count), :]
    for r in range(3):
        arrived(proj_recv.at[r], proj_recv_sem.at[r])
        total = total + proj_recv[r].astype(jnp.float32)
    projected_out[...] = total
    loads[2].wait()
    loads[3].wait()
    one, two = moments(total, moment_one[...], moment_two[...])
    step_out[...] = (
        one / bias_one / (jnp.sqrt(two / bias_two) + adam_epsilon)
    ).astype(step_out.dtype)

    for i in range(own):
        for slot in range(SQUARE):
            @pl.when(core * own + i != place)
            def _():
                arrived(final_tiles.at[i, column(slot)], final_recv.at[i, slot])

            @pl.when(core * own + i == place)
            def _():
                keep_final(i, slot).wait()

    for s in range(1, line):
        coords_copy(s).wait_send()
    for slot in (1, 2):
        for k in range(4):
            row_copy(slot, k).wait_send()
    for k in range(4):
        far_copy(k).wait_send()
    for s in range(line):
        for p in range(PARTS):
            for way, here, z, on in (
                (0, place - s >= 0, place - s, place + 1 < line),
                (1, place + s < line, place + s, place > 0),
            ):
                @pl.when(here & on)
                def _():
                    line_copy(token_piece(z, p), z, p, way).wait_send()
    for r, dp in ((1, side_x), (2, side_y), (3, far)):
        remote(
            proj_send.at[dp - place * SQUARE], proj_recv.at[r - 1],
            proj_send_sem.at[r - 1], proj_recv_sem.at[r - 1], dp, core,
        ).wait_send()
    for i in range(own):
        for slot in range(SQUARE):
            pair_copy(i, slot).wait_send()

            @pl.when(core * own + i != place)
            def _():
                final_copy(i, slot).wait_send()


def direction_kernel(
    step_dir, projected, moment_one, moment_two, basis, tiles,
    new_one, new_two, direction, feature_grad,
):
    for i in range(tiles.shape[0]):
        feature_grad[:, pl.ds(i * tiles.shape[2], tiles.shape[2])] = tiles[i]
    direction[...] = lax.dot_general(
        step_dir[...], basis[...], NT, preferred_element_type=jnp.float32
    )

    @pl.when(pl.program_id(0) == 1)
    def _():
        new_one[...], new_two[...] = moments(projected[...], moment_one[...], moment_two[...])


def fused_body(n_dp, n_tensor, features, out_grad, weight, basis, moment_one, moment_two):
    line = n_dp // SQUARE
    own = line // n_tensor
    n_tok, width = out_grad.shape
    n_row = weight.shape[0]
    units, rank = moment_one.shape[1:]
    dma = pltpu.SemaphoreType.DMA
    bf16, f32 = jnp.bfloat16, jnp.float32
    tiles, projected, step_dir = pl.pallas_call(
        functools.partial(exchange_kernel, line, n_tensor),
        out_shape=(
            jax.ShapeDtypeStruct((own, SQUARE, n_tok, n_row), bf16),
            jax.ShapeDtypeStruct((units, rank), f32),
            jax.ShapeDtypeStruct((units, rank), bf16),
        ),
        in_specs=[pl.BlockSpec(memory_space=pltpu.HBM)] * 6,
        out_specs=[
            pl.BlockSpec(memory_space=pl.ANY),
            pl.BlockSpec(memory_space=pltpu.VMEM),
            pl.BlockSpec(memory_space=pltpu.VMEM),
        ],
        scratch_shapes=[
            pltpu.VMEM(features.shape, bf16),
            pltpu.VMEM(basis.shape, bf16),
            pltpu.VMEM((units, rank), f32),
            pltpu.VMEM((units, rank), f32),
            pltpu.VMEM((line * n_tok, width), bf16),
            pltpu.VMEM((SQUARE, n_row, width), bf16),
            pltpu.VMEM((line, n_tok, rank), bf16),
            pltpu.VMEM((2, n_tok, rank), f32),
            pltpu.VMEM((line, SQUARE, n_tok, n_row), bf16),
            pltpu.VMEM((own, SQUARE, n_tok, n_row), bf16),
            pltpu.VMEM((SQUARE * units, rank), f32),
            pltpu.VMEM((SQUARE, units, rank), bf16),
            pltpu.VMEM((SQUARE - 1, units, rank), bf16),
            dma((6,)),
            dma((2, line, PARTS)),
            dma((line, PARTS)),
            dma((2, 4)),
            dma((2, 4)),
            dma((4,)),
            dma((4,)),
            dma((1,)),
            dma((1,)),
            dma((line,)),
            dma((line,)),
            dma((SQUARE - 1,)),
            dma((SQUARE - 1,)),
            dma((own, SQUARE)),
            dma((own, SQUARE)),
            dma((own, SQUARE)),
            dma((own, SQUARE)),
            dma((SQUARE,)),
        ],
        compiler_params=pltpu.CompilerParams(
            collective_id=0, has_side_effects=True, vmem_limit_bytes=64 << 20
        ),
        name="exchange",
    )(features, out_grad, weight, basis, moment_one[0], moment_two[0])

    n_feature = basis.shape[0]
    block = n_feature // 4
    whole = pl.BlockSpec((units, rank), lambda i: (0, 0))
    count = own * SQUARE // 4
    new_one, new_two, direction, feature_grad = pl.pallas_call(
        direction_kernel,
        grid=(n_feature // block,),
        out_shape=(
            jax.ShapeDtypeStruct((units, rank), f32),
            jax.ShapeDtypeStruct((units, rank), f32),
            jax.ShapeDtypeStruct((units, n_feature), f32),
            jax.ShapeDtypeStruct(features.shape, bf16),
        ),
        in_specs=[
            whole, whole, whole, whole,
            pl.BlockSpec((block, rank), lambda i: (i, 0)),
            pl.BlockSpec((count, n_tok, n_row), lambda i: (i, 0, 0)),
        ],
        out_specs=[
            whole, whole,
            pl.BlockSpec((units, block), lambda i: (0, i)),
            pl.BlockSpec((n_tok, count * n_row), lambda i: (0, i)),
        ],
        compiler_params=pltpu.CompilerParams(vmem_limit_bytes=64 << 20),
        name="direction",
    )(step_dir, projected, moment_one[0], moment_two[0], basis, tiles.reshape(own * SQUARE, n_tok, n_row))
    return (feature_grad, new_one[None], new_two[None], direction[None])


def gathered_body(features, out_grad, weight, basis, moment_one, moment_two):
    partial_value = jnp.einsum(
        "tf,df->td",
        out_grad,
        lax.all_gather(weight, "dp", axis=0, tiled=True),
        preferred_element_type=jnp.float32,
    )
    feature_grad = lax.psum_scatter(
        partial_value.astype(jnp.bfloat16), "tensor", scatter_dimension=1, tiled=True
    )
    part_width = features.shape[1]
    basis_part = lax.dynamic_slice_in_dim(
        basis, lax.axis_index("tensor") * part_width, part_width, 0
    )
    local_coords = jnp.dot(features, basis_part, preferred_element_type=jnp.float32)
    coords = lax.psum(local_coords, "tensor")
    coords = coords.astype(jnp.bfloat16)
    projected = lax.psum_scatter(
        jnp.einsum("tf,tr->fr", out_grad, coords, preferred_element_type=jnp.float32),
        "dp",
        scatter_dimension=0,
        tiled=True,
    )
    first = moment_one[0]
    second = moment_two[0]
    new_one = beta_one * first + (1.0 - beta_one) * projected
    new_two = beta_two * second + (1.0 - beta_two) * projected * projected
    step_dir = (new_one / bias_one / (jnp.sqrt(new_two / bias_two) + adam_epsilon)).astype(
        jnp.bfloat16
    )
    direction = jnp.einsum("cr,dr->cd", step_dir, basis, preferred_element_type=jnp.float32)
    return (feature_grad, new_one[None], new_two[None], direction[None])


def body(n_dp, n_tensor, *arrays):
    _, out_grad, weight, basis, moment_one, _ = arrays
    line = n_dp // SQUARE
    units = moment_one.shape[1]
    fits = (
        n_tensor == 2
        and n_dp % SQUARE == 0
        and line % n_tensor == 0
        and out_grad.shape[1] % 256 == 0
        and out_grad.shape[0] % (16 * PARTS) == 0
        and weight.shape[0] % 128 == 0
        and units % 16 == 0
        and basis.shape[0] % 512 == 0
        and (units * SQUARE) % 128 == 0
    )
    if fits:
        return fused_body(n_dp, n_tensor, *arrays)
    return gathered_body(*arrays)


def solution(mesh):
    in_specs = (
        P("dp", "tensor"),
        P("dp", "tensor"),
        P("dp", "tensor"),
        P(),
        P("tensor", "dp", None),
        P("tensor", "dp", None),
    )
    out_specs = (
        P("dp", "tensor"),
        P("tensor", "dp", None),
        P("tensor", "dp", None),
        P("tensor", "dp", None),
    )
    run = functools.partial(body, mesh.shape["dp"], mesh.shape["tensor"])
    return jax.shard_map(run, mesh=mesh, in_specs=in_specs, out_specs=out_specs, check_vma=False)
```

```python
import functools

import jax
import jax.numpy as jnp
from jax import lax
from jax.experimental import pallas as pl
from jax.experimental.pallas import tpu as pltpu
from jax.sharding import PartitionSpec as P

beta_one = 0.9
beta_two = 0.95
bias_one = 1.0 - 0.9**20
bias_two = 1.0 - 0.95**20
adam_epsilon = 1e-08

MESH = pl.DeviceIdType.MESH
SQUARE = 4
PARTS = 4
WINDOW = 3
NT = (((1,), (1,)), ((), ()))
TN = (((0,), (0,)), ((), ()))


def moments(projected, moment_one, moment_two):
    return (
        beta_one * moment_one + (1.0 - beta_one) * projected,
        beta_two * moment_two + (1.0 - beta_two) * projected * projected,
    )


def exchange_kernel(
    line, n_tensor,
    features_in, out_grad, weight, basis_in, moment_one_in, moment_two_in,
    final_tiles, projected_out, step_out,
    features, basis, moment_one, moment_two, tokens, rows, coords, coords_part, tiles, pair_tiles, proj, proj_send, proj_recv,
    local_sem, line_send, line_recv, row_send, row_recv, far_send, far_recv,
    part_send, part_recv, coords_send, coords_recv,
    proj_send_sem, proj_recv_sem, pair_send, pair_recv, final_send, final_recv, keep_sem,
):
    me = lax.axis_index("dp")
    core = lax.axis_index("tensor")
    place = me // SQUARE
    corner = me % SQUARE
    side_x = place * SQUARE + corner + 1 - 2 * (corner % 2)
    side_y = place * SQUARE + corner + 2 - 4 * (corner // 2)
    far = place * SQUARE + (SQUARE - 1 - corner)
    other = 1 - core
    n_tok = out_grad.shape[0]
    width = out_grad.shape[1]
    n_row = weight.shape[0]
    quarter = n_row // 4
    piece = n_tok // PARTS
    own = line // n_tensor

    def on_line(z):
        return z * SQUARE + corner

    def remote(src, dst, send, recv, dp, tensor):
        return pltpu.make_async_remote_copy(
            src_ref=src, dst_ref=dst, send_sem=send, recv_sem=recv,
            device_id=(dp, tensor), device_id_type=MESH,
        )

    def arrived(dst, sem):
        remote(dst, dst, sem, sem, me, other).wait_recv()

    def token_piece(z, p):
        return tokens.at[pl.ds(pl.multiple_of(z * n_tok + p * piece, piece), piece), :]

    keep_tokens = pltpu.make_async_copy(
        out_grad, tokens.at[pl.ds(pl.multiple_of(place * n_tok, n_tok), n_tok), :], local_sem.at[0]
    )
    keep_rows = pltpu.make_async_copy(weight, rows.at[0], local_sem.at[1])
    loads = [
        pltpu.make_async_copy(src, dst, local_sem.at[2 + i])
        for i, (src, dst) in enumerate(
            (
                (features_in, features),
                (basis_in, basis),
                (moment_one_in, moment_one),
                (moment_two_in, moment_two),
            )
        )
    ]
    for load in loads[:2]:
        load.start()
    keep_tokens.start()
    keep_rows.start()
    for load in loads[2:]:
        load.start()

    barrier = pltpu.get_barrier_semaphore()
    greeted = [(me, other), (side_x, core), (side_y, core), (far, core)]
    for s in range(1, line):
        for t in range(n_tensor):
            greeted.append((on_line((place + s) % line), t))
    for dp, t in greeted:
        pl.semaphore_signal(barrier, inc=1, device_id=(dp, t), device_id_type=MESH)
    pl.semaphore_wait(barrier, len(greeted))

    def line_copy(src, z, p, way):
        target = on_line(place + 1 if way == 0 else place - 1)
        return remote(
            src, token_piece(z, p), line_send.at[way, z, p], line_recv.at[z, p], target, core
        )

    def send_own(p):
        for way, there in ((0, place + 1 < line), (1, place > 0)):
            @pl.when(there)
            def _():
                line_copy(out_grad.at[pl.ds(p * piece, piece), :], place, p, way).start()

    for p in range(WINDOW):
        send_own(p)

    def row_copy(slot, k):
        return remote(
            weight.at[pl.ds(k * quarter, quarter), :],
            rows.at[slot, pl.ds(k * quarter, quarter), :],
            row_send.at[slot - 1, k], row_recv.at[slot - 1, k],
            side_x if slot == 1 else side_y, core,
        )

    def far_copy(k):
        src = rows.at[1 + k // 2, pl.ds(k * quarter, quarter), :]
        return remote(
            src, rows.at[3, pl.ds(k * quarter, quarter), :], far_send.at[k], far_recv.at[k],
            side_y if k < 2 else side_x, core,
        )

    for slot, k in ((1, 0), (2, 2), (1, 1), (2, 3), (1, 2), (2, 0)):
        row_copy(slot, k).start()

    depth = features.shape[1]
    loads[0].wait()
    loads[1].wait()
    coords_part[0] = jnp.dot(
        features[...],
        basis[pl.ds(pl.multiple_of(core * depth, depth), depth), :],
        preferred_element_type=jnp.float32,
    )
    part_copy = remote(
        coords_part.at[0], coords_part.at[1], part_send.at[0], part_recv.at[0], me, other
    )
    part_copy.start()
    part_copy.wait()
    coords[place] = (coords_part[0] + coords_part[1]).astype(coords.dtype)

    def coords_copy(s):
        z = (place + s) % line
        return remote(
            coords.at[place], coords.at[place], coords_send.at[s], coords_recv.at[place],
            on_line(z), core,
        )

    for s in range(1, line):
        coords_copy(s).start()
    keep_tokens.wait()
    keep_rows.wait()

    strip = SQUARE * projected_out.shape[0]

    def add_projected(z, first=False):
        block = tokens[
            pl.ds(pl.multiple_of(z * n_tok, n_tok), n_tok),
            pl.ds(pl.multiple_of(place * strip, strip), strip),
        ]
        term = lax.dot_general(block, coords[z], TN, preferred_element_type=jnp.float32)
        proj[...] = term if first else proj[...] + term

    def product(first_token, count, slot):
        return lax.dot_general(
            tokens[pl.ds(first_token, count), :], rows[slot], NT,
            preferred_element_type=jnp.float32,
        )

    def column(slot):
        flip_x = slot % 2
        flip_y = slot // 2
        x, y = corner % 2, corner // 2
        return (x + flip_x) % 2 + 2 * ((y + flip_y) % 2)

    def tile(z, slot):
        got = product(pl.multiple_of(z * n_tok, n_tok), n_tok, slot)
        tiles[z, column(slot)] = got.astype(tiles.dtype)

    def tiles_of(z, slots):
        def one(slot, carry):
            tile(z, slot)
            return carry

        lax.fori_loop(slots[0], slots[1], one, 0)

    def far_tiles(z):
        block = tokens[pl.ds(pl.multiple_of(z * n_tok, n_tok), n_tok), :]
        got = lax.dot_general(
            block, rows[0:3].reshape(3 * n_row, width), NT, preferred_element_type=jnp.float32
        )
        for slot in range(3):
            tiles[z, column(slot)] = got[:, slot * n_row : (slot + 1) * n_row].astype(tiles.dtype)

    add_projected(place, first=True)
    tile(place, 0)

    late = max(line - 2, 1)
    mine = place // own

    def pair_copy(i, slot):
        c = column(slot)
        return remote(
            tiles.at[other * own + i, c], pair_tiles.at[i, c],
            pair_send.at[i, slot], pair_recv.at[i, slot], me, other,
        )

    def final_copy(i, slot):
        c = column(slot)
        return remote(
            pair_tiles.at[i, c], final_tiles.at[place % own, c],
            final_send.at[i, slot], final_recv.at[place % own, slot],
            on_line(core * own + i), mine,
        )

    def keep_final(i, slot):
        c = column(slot)
        return pltpu.make_async_copy(
            pair_tiles.at[i, c], final_tiles.at[place % own, c], keep_sem.at[slot]
        )

    def near(z):
        return (z - place <= late) & (place - z <= late)

    def finish(i, slot):
        c = column(slot)
        pair_copy(i, slot).wait_recv()
        z = core * own + i
        pair_tiles[i, c] = (
            tiles[z, c].astype(jnp.float32) + pair_tiles[i, c].astype(jnp.float32)
        ).astype(pair_tiles.dtype)

        @pl.when(z == place)
        def _():
            keep_final(i, slot).start()

        @pl.when(z != place)
        def _():
            final_copy(i, slot).start()

    def early_slots(now):
        for i in range(own):
            @pl.when(near(other * own + i) == now)
            def _():
                for slot in range(SQUARE - 1):
                    pair_copy(i, slot).start()

        for i in range(own):
            @pl.when(near(core * own + i) == now)
            def _():
                for slot in range(SQUARE - 1):
                    finish(i, slot)

    for s in range(1, line):
        from_left = place - s >= 0
        from_right = place + s < line
        for p in range(PARTS):
            for way, here, z, on in (
                (0, from_left, place - s, place + 1 < line),
                (1, from_right, place + s, place > 0),
            ):
                @pl.when(here)
                def _():
                    arrived(token_piece(z, p), line_recv.at[z, p])

                    @pl.when(on)
                    def _():
                        line_copy(token_piece(z, p), z, p, way).start()

            if s == 1 and p + WINDOW < PARTS:
                send_own(p + WINDOW)

        if s == 1:
            row_copy(1, 3).start()
            row_copy(2, 1).start()
        for here, z in ((from_left, place - s), (from_right, place + s)):
            @pl.when(here)
            def _():
                arrived(coords.at[z], coords_recv.at[z])
                add_projected(z)

        if s == line - 1:
            for r in range(SQUARE):
                proj_send[r] = proj[
                    pl.ds(r * projected_out.shape[0], projected_out.shape[0]), :
                ].astype(proj_send.dtype)
            for r, dp in ((1, side_x), (2, side_y), (3, far)):
                remote(
                    proj_send.at[dp - place * SQUARE], proj_recv.at[r - 1],
                    proj_send_sem.at[r - 1], proj_recv_sem.at[r - 1], dp, core,
                ).start()

        for here, z in ((from_left, place - s), (from_right, place + s)):
            @pl.when(here)
            def _():
                if s > late:
                    far_tiles(z)
                else:
                    tile(z, 0)

        if s == 1:
            for k in (0, 2, 1, 3):
                slot = 1 + k // 2
                arrived(rows.at[slot, pl.ds(k * quarter, quarter), :], row_recv.at[slot - 1, k])
                far_copy(k).start()

        if s == late:
            for slot, k in ((1, 2), (2, 0), (1, 3), (2, 1)):
                arrived(rows.at[slot, pl.ds(k * quarter, quarter), :], row_recv.at[slot - 1, k])

            def early(z, carry):
                @pl.when(near(z))
                def _():
                    tiles_of(z, (1, 3))

                return carry

            lax.fori_loop(0, line, early, 0)
            early_slots(True)

    early_slots(False)

    for k in range(4):
        arrived(rows.at[3, pl.ds(k * quarter, quarter), :], far_recv.at[k])

    def last(t):
        got = product(pl.multiple_of(t * own * n_tok, own * n_tok), own * n_tok, 3)
        for i in range(own):
            tiles[t * own + i, column(3)] = got[i * n_tok : (i + 1) * n_tok].astype(tiles.dtype)

    last(other)
    for i in range(own):
        pair_copy(i, 3).start()
    last(core)
    for i in range(own):
        finish(i, 3)

    count = projected_out.shape[0]
    total = proj[pl.ds(pl.multiple_of(corner * count, count), count), :]
    for r in range(3):
        arrived(proj_recv.at[r], proj_recv_sem.at[r])
        total = total + proj_recv[r].astype(jnp.float32)
    projected_out[...] = total
    loads[2].wait()
    loads[3].wait()
    one, two = moments(total, moment_one[...], moment_two[...])
    step_out[...] = (
        one / bias_one / (jnp.sqrt(two / bias_two) + adam_epsilon)
    ).astype(step_out.dtype)

    for i in range(own):
        for slot in range(SQUARE):
            @pl.when(core * own + i != place)
            def _():
                arrived(final_tiles.at[i, column(slot)], final_recv.at[i, slot])

            @pl.when(core * own + i == place)
            def _():
                keep_final(i, slot).wait()

    for s in range(1, line):
        coords_copy(s).wait_send()
    for slot in (1, 2):
        for k in range(4):
            row_copy(slot, k).wait_send()
    for k in range(4):
        far_copy(k).wait_send()
    for s in range(line):
        for p in range(PARTS):
            for way, here, z, on in (
                (0, place - s >= 0, place - s, place + 1 < line),
                (1, place + s < line, place + s, place > 0),
            ):
                @pl.when(here & on)
                def _():
                    line_copy(token_piece(z, p), z, p, way).wait_send()
    for r, dp in ((1, side_x), (2, side_y), (3, far)):
        remote(
            proj_send.at[dp - place * SQUARE], proj_recv.at[r - 1],
            proj_send_sem.at[r - 1], proj_recv_sem.at[r - 1], dp, core,
        ).wait_send()
    for i in range(own):
        for slot in range(SQUARE):
            pair_copy(i, slot).wait_send()

            @pl.when(core * own + i != place)
            def _():
                final_copy(i, slot).wait_send()


def direction_kernel(
    step_dir, projected, moment_one, moment_two, basis, tiles,
    new_one, new_two, direction, feature_grad,
):
    for i in range(tiles.shape[0]):
        feature_grad[:, pl.ds(i * tiles.shape[2], tiles.shape[2])] = tiles[i]
    direction[...] = lax.dot_general(
        step_dir[...], basis[...], NT, preferred_element_type=jnp.float32
    )

    @pl.when(pl.program_id(0) == 1)
    def _():
        new_one[...], new_two[...] = moments(projected[...], moment_one[...], moment_two[...])


def fused_body(n_dp, n_tensor, features, out_grad, weight, basis, moment_one, moment_two):
    line = n_dp // SQUARE
    own = line // n_tensor
    n_tok, width = out_grad.shape
    n_row = weight.shape[0]
    units, rank = moment_one.shape[1:]
    dma = pltpu.SemaphoreType.DMA
    bf16, f32 = jnp.bfloat16, jnp.float32
    tiles, projected, step_dir = pl.pallas_call(
        functools.partial(exchange_kernel, line, n_tensor),
        out_shape=(
            jax.ShapeDtypeStruct((own, SQUARE, n_tok, n_row), bf16),
            jax.ShapeDtypeStruct((units, rank), f32),
            jax.ShapeDtypeStruct((units, rank), bf16),
        ),
        in_specs=[pl.BlockSpec(memory_space=pltpu.HBM)] * 6,
        out_specs=[
            pl.BlockSpec(memory_space=pl.ANY),
            pl.BlockSpec(memory_space=pltpu.VMEM),
            pl.BlockSpec(memory_space=pltpu.VMEM),
        ],
        scratch_shapes=[
            pltpu.VMEM(features.shape, bf16),
            pltpu.VMEM(basis.shape, bf16),
            pltpu.VMEM((units, rank), f32),
            pltpu.VMEM((units, rank), f32),
            pltpu.VMEM((line * n_tok, width), bf16),
            pltpu.VMEM((SQUARE, n_row, width), bf16),
            pltpu.VMEM((line, n_tok, rank), bf16),
            pltpu.VMEM((2, n_tok, rank), f32),
            pltpu.VMEM((line, SQUARE, n_tok, n_row), bf16),
            pltpu.VMEM((own, SQUARE, n_tok, n_row), bf16),
            pltpu.VMEM((SQUARE * units, rank), f32),
            pltpu.VMEM((SQUARE, units, rank), bf16),
            pltpu.VMEM((SQUARE - 1, units, rank), bf16),
            dma((6,)),
            dma((2, line, PARTS)),
            dma((line, PARTS)),
            dma((2, 4)),
            dma((2, 4)),
            dma((4,)),
            dma((4,)),
            dma((1,)),
            dma((1,)),
            dma((line,)),
            dma((line,)),
            dma((SQUARE - 1,)),
            dma((SQUARE - 1,)),
            dma((own, SQUARE)),
            dma((own, SQUARE)),
            dma((own, SQUARE)),
            dma((own, SQUARE)),
            dma((SQUARE,)),
        ],
        compiler_params=pltpu.CompilerParams(
            collective_id=0, has_side_effects=True, vmem_limit_bytes=64 << 20
        ),
        name="exchange",
    )(features, out_grad, weight, basis, moment_one[0], moment_two[0])

    n_feature = basis.shape[0]
    block = n_feature // 4
    whole = pl.BlockSpec((units, rank), lambda i: (0, 0))
    count = own * SQUARE // 4
    new_one, new_two, direction, feature_grad = pl.pallas_call(
        direction_kernel,
        grid=(n_feature // block,),
        out_shape=(
            jax.ShapeDtypeStruct((units, rank), f32),
            jax.ShapeDtypeStruct((units, rank), f32),
            jax.ShapeDtypeStruct((units, n_feature), f32),
            jax.ShapeDtypeStruct(features.shape, bf16),
        ),
        in_specs=[
            whole, whole, whole, whole,
            pl.BlockSpec((block, rank), lambda i: (i, 0)),
            pl.BlockSpec((count, n_tok, n_row), lambda i: (i, 0, 0)),
        ],
        out_specs=[
            whole, whole,
            pl.BlockSpec((units, block), lambda i: (0, i)),
            pl.BlockSpec((n_tok, count * n_row), lambda i: (0, i)),
        ],
        compiler_params=pltpu.CompilerParams(vmem_limit_bytes=64 << 20),
        name="direction",
    )(step_dir, projected, moment_one[0], moment_two[0], basis, tiles.reshape(own * SQUARE, n_tok, n_row))
    return (feature_grad, new_one[None], new_two[None], direction[None])


def gathered_body(features, out_grad, weight, basis, moment_one, moment_two):
    partial_value = jnp.einsum(
        "tf,df->td",
        out_grad,
        lax.all_gather(weight, "dp", axis=0, tiled=True),
        preferred_element_type=jnp.float32,
    )
    feature_grad = lax.psum_scatter(
        partial_value.astype(jnp.bfloat16), "tensor", scatter_dimension=1, tiled=True
    )
    part_width = features.shape[1]
    basis_part = lax.dynamic_slice_in_dim(
        basis, lax.axis_index("tensor") * part_width, part_width, 0
    )
    local_coords = jnp.dot(features, basis_part, preferred_element_type=jnp.float32)
    coords = lax.psum(local_coords, "tensor")
    coords = coords.astype(jnp.bfloat16)
    projected = lax.psum_scatter(
        jnp.einsum("tf,tr->fr", out_grad, coords, preferred_element_type=jnp.float32),
        "dp",
        scatter_dimension=0,
        tiled=True,
    )
    first = moment_one[0]
    second = moment_two[0]
    new_one = beta_one * first + (1.0 - beta_one) * projected
    new_two = beta_two * second + (1.0 - beta_two) * projected * projected
    step_dir = (new_one / bias_one / (jnp.sqrt(new_two / bias_two) + adam_epsilon)).astype(
        jnp.bfloat16
    )
    direction = jnp.einsum("cr,dr->cd", step_dir, basis, preferred_element_type=jnp.float32)
    return (feature_grad, new_one[None], new_two[None], direction[None])


def body(n_dp, n_tensor, *arrays):
    _, out_grad, weight, basis, moment_one, _ = arrays
    line = n_dp // SQUARE
    units = moment_one.shape[1]
    fits = (
        n_tensor == 2
        and n_dp % SQUARE == 0
        and line % n_tensor == 0
        and out_grad.shape[1] % 256 == 0
        and out_grad.shape[0] % (16 * PARTS) == 0
        and weight.shape[0] % 128 == 0
        and units % 16 == 0
        and basis.shape[0] % 512 == 0
        and (units * SQUARE) % 128 == 0
    )
    if fits:
        return fused_body(n_dp, n_tensor, *arrays)
    return gathered_body(*arrays)


def solution(mesh):
    in_specs = (
        P("dp", "tensor"),
        P("dp", "tensor"),
        P("dp", "tensor"),
        P(),
        P("tensor", "dp", None),
        P("tensor", "dp", None),
    )
    out_specs = (
        P("dp", "tensor"),
        P("tensor", "dp", None),
        P("tensor", "dp", None),
        P("tensor", "dp", None),
    )
    run = functools.partial(body, mesh.shape["dp"], mesh.shape["tensor"])
    return jax.shard_map(run, mesh=mesh, in_specs=in_specs, out_specs=out_specs, check_vma=False)
```
